256 devices in a mesh: row: 16 (over z_hi, x), col: 8 (over y, z_lo), feat: 2 (over core).
Axes of the slice: x: 4, y: 4, z: 8 (z_hi: 4, z_lo: 2; z = z_hi * 2 + z_lo), core: 2. Of those that a mesh axis runs over, the one named last changes fastest.
Arguments:
- tile_vals: bfloat16 [16, 8, 384, 128, 128], P('row', 'col'), may hold values from -0.09375 to 0.09375
- tile_rows: int32 [16, 8, 384], P('row', 'col'), may hold values from 0 to 31, as said below
- tile_cols: int32 [16, 8, 384], P('row', 'col'), may hold values from 0 to 63, as said below
- tile_count: int32 [16, 8], P('row', 'col'), may hold values from 1 to 384, as said below
- features: bfloat16 [65536, 256], P(('row', 'col'), 'feat'), may hold values from -6 to 6
- weight: bfloat16 [256, 256], P(None, 'feat'), may hold values from -0.375 to 0.375
- bias_term: float32 [256], P('feat'), may hold values from -3 to 3
- cotangent: bfloat16 [65536, 256], P(('row', 'col'), 'feat'), may hold values from -6 to 6
Outputs:
- outputs: bfloat16 [65536, 256], P(('row', 'col'), 'feat')
- grad_feat: bfloat16 [65536, 256], P(('row', 'col'), 'feat')
- grad_weight: float32 [256, 256], P(None, 'feat')
- grad_bias: float32 [256], P('feat')
The draws below stay inside these ranges and needn't reach their ends.
Inputs may be any that keep to these rules, and one draw needn't show every extreme that they name: Within one grid cell the live slots name distinct tile positions; tile_rows is below 32. tile_cols is below 64; the position of a slot is tile_rows * 64 + tile_cols. `tile_count`: some grid cell has all 384 slots live in every draw.
All inputs are finite; a program needn't handle non-finite values.
Results may differ from the reference program's by a relative error of at most 0.025.
Values may be sent and summed in bfloat16 or wider, within the bound.
No kernel may reach another device: no remote copies, remote signals or barrier semaphores. Data moves between devices by JAX's collectives and lax.ppermute only.
A program may use at most 128 MiB of HBM per device.

```python
import math
import jax
import jax.numpy as jnp
from jax import lax

SPAN = 512
HID = 256
TILE = 128
NODES = 65536
TROWS = 32
TCOLS = 64
TCAP = 384
N_ROW = 16
N_COL = 8


def tile_positions(key):
    cell_keys = jax.random.split(key, N_ROW * N_COL)
    orders = jax.vmap(lambda cell_key: jax.random.permutation(cell_key, TROWS * TCOLS))(cell_keys)
    return orders[:, :TCAP].reshape(N_ROW, N_COL, TCAP).astype(jnp.int32)


def draw_tile_rows(key, part):
    positions = tile_positions(key)
    return (positions // TCOLS).astype(jnp.int32)


def draw_tile_cols(key, part):
    positions = tile_positions(key)
    return (positions % TCOLS).astype(jnp.int32)


def draw_tile_count(key, part):
    key = jax.random.fold_in(key, 3)
    first_key, second_key = jax.random.split(key)
    raw_counts = jax.random.randint(first_key, (N_ROW * N_COL,), 1, TCAP + 1)
    counts = jnp.maximum(raw_counts * raw_counts // TCAP, 1)
    busiest = jax.random.randint(second_key, (), 0, N_ROW * N_COL)
    counts = jnp.where(jnp.arange(N_ROW * N_COL) == busiest, TCAP, counts)
    return counts.reshape(N_ROW, N_COL).astype(jnp.int32)


def block_scale(stream_key, extent, cuts, low, largest):
    def one(position, blocks):
        heights = jax.random.uniform(jax.random.fold_in(jax.random.fold_in(stream_key, 6), position), (blocks,), jnp.float32, low / len(cuts), largest / len(cuts))
        return jnp.repeat(jnp.exp(heights), extent[position] // blocks).reshape((-1,) + (1,) * (len(extent) - position - 1))

    level = one(*cuts[0])
    for cut in cuts[1:]:
        level = level * one(*cut)
    return level


def noise(own_key, shape, width, most, pieces=(), kind=jnp.bfloat16):
    entries = width * jax.random.normal(own_key, shape, jnp.float32)
    if pieces:
        entries = entries * block_scale(own_key, shape, pieces, -0.22, 0.18)
    return jnp.clip(entries, -most, most).astype(kind)


def setup_inputs(seed: int = 0) -> dict:
    splits = jax.random.split(jax.random.key(seed), 9)
    tile_vals = noise(splits[0], (N_ROW, N_COL, TCAP, TILE, TILE), (NODES // 16) ** -0.5, 0.09375, ((0, 16), (1, 8)))
    tile_rows = draw_tile_rows(jax.random.fold_in(splits[8], 71), 0)
    tile_cols = draw_tile_cols(jax.random.fold_in(splits[8], 71), 0)
    tile_count = draw_tile_count(jax.random.fold_in(splits[8], 71), 0)
    features = noise(splits[4], (NODES, HID), 1.0, 6.0, ((0, 128), (1, 2)))
    weight = noise(splits[5], (HID, HID), HID ** -0.5, 0.375, ((1, 2),))
    bias_term = noise(splits[6], (HID,), 0.5, 3.0, ((0, 2),), jnp.float32)
    cotangent = noise(splits[7], (NODES, HID), 1.0, 6.0, ((0, 128), (1, 2)))
    return dict(tile_vals=tile_vals, tile_rows=tile_rows, tile_cols=tile_cols, tile_count=tile_count, features=features, weight=weight, bias_term=bias_term, cotangent=cotangent)


def forward_cell(cell_tiles, out_slots, in_slots, live_count, source, totals):

    def add_tile(slot_index, running):
        product = jnp.dot(cell_tiles[slot_index], source[in_slots[slot_index]], preferred_element_type=jnp.float32)
        return running.at[out_slots[slot_index]].add(product)
    return lax.fori_loop(0, live_count, add_tile, totals)

def backward_cell(cell_tiles, out_slots, in_slots, live_count, source, totals):

    def add_tile(slot_index, running):
        product = jnp.dot(cell_tiles[slot_index].T, source[out_slots[slot_index]], preferred_element_type=jnp.float32)
        return running.at[in_slots[slot_index]].add(product)
    return lax.fori_loop(0, live_count, add_tile, totals)

def reference(tile_vals, tile_rows, tile_cols, tile_count, features, weight, bias_term, cotangent):
    channels = features.shape[1]
    node_total = N_ROW * N_COL * SPAN
    projected = jnp.dot(features, weight, preferred_element_type=jnp.float32).astype(jnp.bfloat16)
    col_sets = projected.reshape(N_ROW, N_COL, SPAN, channels).transpose(1, 0, 2, 3).reshape(N_COL, TCOLS, TILE, channels)

    def row_panel(row_index):

        def one_cell(totals, col_index):
            result = forward_cell(tile_vals[row_index, col_index], tile_rows[row_index, col_index], tile_cols[row_index, col_index], tile_count[row_index, col_index], col_sets[col_index], totals)
            return (result, None)
        start = jnp.zeros((TROWS, TILE, channels), jnp.float32)
        summed, ignored = lax.scan(one_cell, start, jnp.arange(N_COL, dtype=jnp.int32))
        return summed
    summed = lax.map(row_panel, jnp.arange(N_ROW, dtype=jnp.int32)).reshape(node_total, channels)
    pre_act = summed + bias_term[None, :]
    sigmoid_pre = jax.nn.sigmoid(pre_act)
    outputs = (pre_act * sigmoid_pre).astype(jnp.bfloat16)
    slope = sigmoid_pre * (1.0 + pre_act * (1.0 - sigmoid_pre))
    grad_pre = (cotangent.astype(jnp.float32) * slope).astype(jnp.bfloat16)
    row_panels = grad_pre.reshape(N_ROW, TROWS, TILE, channels)

    def col_set(col_index):

        def one_cell(totals, row_index):
            result = backward_cell(tile_vals[row_index, col_index], tile_rows[row_index, col_index], tile_cols[row_index, col_index], tile_count[row_index, col_index], row_panels[row_index], totals)
            return (result, None)
        start = jnp.zeros((TCOLS, TILE, channels), jnp.float32)
        summed_back, ignored = lax.scan(one_cell, start, jnp.arange(N_ROW, dtype=jnp.int32))
        return summed_back
    back = lax.map(col_set, jnp.arange(N_COL, dtype=jnp.int32))
    grad_proj = back.reshape(N_COL, N_ROW, SPAN, channels).transpose(1, 0, 2, 3).reshape(node_total, channels).astype(jnp.bfloat16)
    scale_factor = 1.0 / math.sqrt(node_total)
    grad_weight = jnp.dot(features.T, grad_proj, preferred_element_type=jnp.float32) * scale_factor
    grad_bias = lax.optimization_barrier(jnp.sum(grad_pre.astype(jnp.float32), axis=0)) * scale_factor
    grad_feat = jnp.dot(grad_proj, weight.T, preferred_element_type=jnp.float32).astype(jnp.bfloat16)
    return (outputs, grad_feat, grad_weight, grad_bias)
```

```python
import functools
import math

import jax
import jax.numpy as jnp
from jax import lax
from jax.experimental import pallas as pl
from jax.experimental.pallas import tpu as pltpu
from jax.sharding import Mesh
from jax.sharding import PartitionSpec as P

BF16 = jnp.bfloat16
F32 = jnp.float32
EDGE = 128
CHUNK = 32
DEPTH = 3
VMEM_LIMIT = 40 * 2**20


def shift(value, axis, size, step):
    return lax.ppermute(value, axis, [((i + step) % size, i) for i in range(size)])


def push(value, axis, size, step):
    return lax.ppermute(value, axis, [(i, (i + step) % size) for i in range(size)])


def move_col(value, step_y, step_z, pull):
    pairs = []
    for y in range(4):
        for z in range(2):
            here, there = y * 2 + z, ((y + step_y) % 4) * 2 + (z + step_z) % 2
            pairs.append((there, here) if pull else (here, there))
    return lax.ppermute(value, ("y", "zlo"), pairs)


def tile_kernel(transpose, n_src, n_out, count_ref, out_idx_ref, src_idx_ref, tiles_hbm, *refs):
    src_refs = refs[:n_src]
    out_refs = refs[n_src : n_src + n_out]
    buf, sem, source, acc = refs[n_src + n_out :]
    live = count_ref[0]
    chunks = (live + CHUNK - 1) // CHUNK

    def fetch(index, slot):
        return pltpu.make_async_copy(
            tiles_hbm.at[pl.ds(index * CHUNK, CHUNK)], buf.at[slot], sem.at[slot]
        )

    for k in range(DEPTH - 1):

        @pl.when(k < chunks)
        def _():
            fetch(k, k).start()

    per = src_refs[0].shape[0] // EDGE
    for k in range(n_src):
        source[k * per : (k + 1) * per] = src_refs[k][...].reshape(per, EDGE, EDGE)
    acc[...] = jnp.zeros_like(acc)

    def one_chunk(index, carry):
        slot = lax.rem(index, DEPTH)

        @pl.when(index + DEPTH - 1 < chunks)
        def _():
            fetch(index + DEPTH - 1, lax.rem(index + DEPTH - 1, DEPTH)).start()

        fetch(index, slot).wait()
        for k in range(CHUNK):
            place = index * CHUNK + k
            out_at = out_idx_ref[place]
            src_at = src_idx_ref[place]
            tile = buf[slot, k]
            dims = (((0,), (0,)), ((), ())) if transpose else (((1,), (0,)), ((), ()))
            acc[out_at] += lax.dot_general(
                tile, source[src_at], dims, preferred_element_type=F32
            )
        return carry

    lax.fori_loop(0, chunks, one_chunk, 0)
    per = out_refs[0].shape[0] // EDGE
    for k in range(n_out):
        out_refs[k][...] = acc[k * per : (k + 1) * per].reshape(per * EDGE, EDGE).astype(BF16)


def tile_pass(tiles, out_idx, src_idx, count, sources, n_out, out_rows, transpose, name):
    n_src = len(sources)
    src_tiles = n_src * sources[0].shape[0] // EDGE
    out_tiles = n_out * out_rows // EDGE
    smem = pl.BlockSpec(memory_space=pltpu.SMEM)
    vmem = pl.BlockSpec(memory_space=pltpu.VMEM)
    return pl.pallas_call(
        functools.partial(tile_kernel, transpose, n_src, n_out),
        out_shape=[jax.ShapeDtypeStruct((out_rows, EDGE), BF16)] * n_out,
        in_specs=[smem, smem, smem, pl.BlockSpec(memory_space=pl.ANY)] + [vmem] * n_src,
        out_specs=[vmem] * n_out,
        scratch_shapes=[
            pltpu.VMEM((DEPTH, CHUNK, EDGE, EDGE), BF16),
            pltpu.SemaphoreType.DMA((DEPTH,)),
            pltpu.VMEM((src_tiles, EDGE, EDGE), BF16),
            pltpu.VMEM((out_tiles + 1, EDGE, EDGE), F32),
        ],
        compiler_params=pltpu.CompilerParams(vmem_limit_bytes=VMEM_LIMIT),
        name=name,
    )(count, out_idx, src_idx, tiles, *sources)


def sum_kernel(*refs):
    total = refs[0][...].astype(F32)
    for ref in refs[1:-1]:
        total = total + ref[...].astype(F32)
    refs[-1][...] = total.astype(refs[-1].dtype)


def sum_blocks(blocks, dtype, name):
    vmem = pl.BlockSpec(memory_space=pltpu.VMEM)
    return pl.pallas_call(
        sum_kernel,
        out_shape=jax.ShapeDtypeStruct(blocks[0].shape, dtype),
        in_specs=[vmem] * len(blocks),
        out_specs=vmem,
        compiler_params=pltpu.CompilerParams(vmem_limit_bytes=VMEM_LIMIT),
        name=name,
    )(*blocks)


def middle_kernel(
    feat_ref, agg_ref, w_ref, bias_ref, cot_ref, out_ref, hid_ref, gw_ref, grad_own
):
    half = EDGE
    lane = pl.multiple_of(feat_ref[0] * half, half)
    agg = agg_ref[...]
    pre = jnp.dot(agg, w_ref[...], preferred_element_type=F32) + bias_ref[...]
    sig = jax.nn.sigmoid(pre)
    value = (pre * sig).astype(BF16)
    slope = sig * (1.0 + pre * (1.0 - sig))
    grad = (cot_ref[...].astype(F32) * slope).astype(BF16)

    @pl.when(feat_ref[0] == 0)
    def _():
        out_ref[...] = value[:, :half]
        grad_own[...] = grad[:, :half]

    @pl.when(feat_ref[0] == 1)
    def _():
        out_ref[...] = value[:, half:]
        grad_own[...] = grad[:, half:]

    w_rows = w_ref[pl.ds(lane, half), :]
    hid_ref[...] = lax.dot_general(
        grad, w_rows, (((1,), (1,)), ((), ())), preferred_element_type=F32
    ).astype(BF16)
    own = grad_own[...]
    gw_ref[0:256, :] = lax.dot_general(
        agg, own, (((0,), (0,)), ((), ())), preferred_element_type=F32
    )
    gw_ref[256:264, :] = jnp.sum(own.astype(F32).reshape(-1, 8, half), axis=0)


def middle(feat, agg, w_all, bias_all, cot_all):
    rows = agg.shape[0]
    vmem = pl.BlockSpec(memory_space=pltpu.VMEM)
    return pl.pallas_call(
        middle_kernel,
        out_shape=[
            jax.ShapeDtypeStruct((rows, EDGE), BF16),
            jax.ShapeDtypeStruct((rows, EDGE), BF16),
            jax.ShapeDtypeStruct((264, EDGE), F32),
        ],
        in_specs=[pl.BlockSpec(memory_space=pltpu.SMEM)] + [vmem] * 4,
        out_specs=[vmem] * 3,
        scratch_shapes=[pltpu.VMEM((rows, EDGE), BF16)],
        compiler_params=pltpu.CompilerParams(vmem_limit_bytes=VMEM_LIMIT),
        name="middle",
    )(feat, agg, w_all, bias_all, cot_all)


def on_device(tile_vals, tile_rows, tile_cols, tile_count, features, weight, bias_term, cotangent):
    tiles = tile_vals[0, 0]
    rows = tile_rows[0, 0]
    cols = tile_cols[0, 0]
    count = tile_count[0, 0]
    local_rows = features.shape[0]
    my_zhi, my_x = lax.axis_index("zhi"), lax.axis_index("x")
    my_y, my_zlo = lax.axis_index("y"), lax.axis_index("zlo")
    feat = lax.axis_index("feat").reshape(1)

    per = local_rows // EDGE
    row_block, col_block = rows // per, cols // per
    rel_row = ((row_block // 2 - my_y) % 4) * 2 + (row_block % 2 - my_zlo) % 2
    rel_col = ((col_block // 4 - my_zhi) % 4) * 4 + (col_block % 4 - my_x) % 4
    row_at = rel_row * per + rows % per
    col_at = rel_col * per + cols % per
    slots = tiles.shape[0]
    dead = jnp.arange(slots, dtype=jnp.int32) >= count
    row_out = jnp.where(dead, 32, row_at)
    col_out = jnp.where(dead, 64, col_at)
    live = count.reshape(1)

    w_all = lax.all_gather(weight, "feat", axis=1, tiled=True)
    cot_all = lax.all_gather(cotangent, "feat", axis=1, tiled=True)
    bias_all = lax.all_gather(bias_term.reshape(1, -1), "feat", axis=1, tiled=True)

    with jax.named_scope("gather_row"):
        along_z = [features] + [shift(features, "zhi", 4, k) for k in (1, 2, 3)]
        blocks = []
        for block in along_z:
            blocks += [block] + [shift(block, "x", 4, k) for k in (1, 2, 3)]
    partial_sums = tile_pass(tiles, row_out, col_at, live, blocks, 8, local_rows, False, "forward")

    with jax.named_scope("scatter_col"):
        mine = [partial_sums[0]]
        for k in range(1, 8):
            mine.append(move_col(partial_sums[k], k // 2, k % 2, False))
    agg_own = sum_blocks(mine, BF16, "sum_col")
    agg = lax.all_gather(agg_own, "feat", axis=1, tiled=True)
    outputs, hidden, grads = middle(feat, agg, w_all, bias_all, cot_all)

    with jax.named_scope("gather_col"):
        blocks = [hidden]
        for k in range(1, 8):
            blocks.append(move_col(hidden, k // 2, k % 2, True))
    back = tile_pass(tiles, col_out, row_at, live, blocks, 16, local_rows, True, "backward")

    with jax.named_scope("weight_grads"):
        for axis, size in (("x", 4), ("zhi", 4), ("y", 4), ("zlo", 2)):
            got = [shift(grads, axis, size, k) for k in range(1, size)]
            grads = grads + got[0] if size == 2 else (grads + got[1]) + (got[0] + got[2])

    with jax.named_scope("scatter_row"):
        final = []
        for z in (2, 1, 3, 0):
            got = [back[z * 4]] + [push(back[z * 4 + k], "x", 4, k) for k in (1, 2, 3)]
            block = sum_blocks(got, BF16 if z else F32, "sum_x")
            final.append(push(block, "zhi", 4, z) if z else block)
    grad_feat = sum_blocks(final, BF16, "sum_z")

    node_total = local_rows * 128
    scale = 1.0 / math.sqrt(node_total)
    return (
        outputs,
        grad_feat,
        grads[:256] * scale,
        jnp.sum(grads[256:], axis=0) * scale,
    )


def solution(mesh):
    fine = Mesh(mesh.devices.reshape(4, 4, 4, 2, 2), ("zhi", "x", "y", "zlo", "feat"))
    row, col = ("zhi", "x"), ("y", "zlo")
    nodes = P(row + col, "feat")
    return jax.shard_map(
        on_device,
        mesh=fine,
        in_specs=(
            P(row, col, None, None, None),
            P(row, col, None),
            P(row, col, None),
            P(row, col),
            nodes,
            P(None, "feat"),
            P("feat"),
            nodes,
        ),
        out_specs=(nodes, nodes, P(None, "feat"), P("feat")),
        check_vma=False,
    )
```

```python
import functools
import math

import jax
import jax.numpy as jnp
from jax import lax
from jax.experimental import pallas as pl
from jax.experimental.pallas import tpu as pltpu
from jax.sharding import Mesh
from jax.sharding import PartitionSpec as P

BF16 = jnp.bfloat16
F32 = jnp.float32
EDGE = 128
CHUNK = 32
DEPTH = 3
HALF_TILES = 32
VMEM_LIMIT = 40 * 2**20


def pull(value, axis, size, step):
    return lax.ppermute(value, axis, [((i + step) % size, i) for i in range(size)])


def push(value, axis, size, step):
    return lax.ppermute(value, axis, [(i, (i + step) % size) for i in range(size)])


def push_col(value, step_y, step_z):
    pairs = []
    for y in range(4):
        for z in range(2):
            pairs.append((y * 2 + z, ((y + step_y) % 4) * 2 + (z + step_z) % 2))
    return lax.ppermute(value, ("y", "zlo"), pairs)


def group_sum(value, axis, size):
    with jax.named_scope("weight_grads"):
        parts = [pull(value, axis, size, k) for k in range(1, size)]
        if size == 2:
            return value + parts[0]
        return (value + parts[1]) + (parts[0] + parts[2])


def slot_lists(rows, cols, second, live):
    slots = rows.shape[0]
    index = jnp.arange(slots, dtype=jnp.int32)
    code = index * 4096 + rows * 64 + cols
    kind = jnp.stack([jnp.logical_not(second), second]) & (index < live)[None]
    before = index[None, :] < index[:, None]
    rank = jnp.sum((kind[:, None, :] & before[None]).astype(jnp.int32), axis=2)
    hit = kind[:, None, :] & (rank[:, None, :] == index[None, :, None])
    packed = jnp.sum(jnp.where(hit, code[None, None, :], 0), axis=2)
    totals = jnp.sum(kind.astype(jnp.int32), axis=1)
    packed = jnp.where(index[None] < totals[:, None], packed, 32 * 64 + 32)
    return packed, totals


def tile_kernel(transpose, n_src, n_out, has_base, total_ref, list_ref, tiles_hbm, *refs):
    src_refs = refs[:n_src]
    base = refs[n_src] if has_base else None
    n_in = n_src + has_base
    out_refs = refs[n_in : n_in + n_out]
    buf, sem, source, acc = refs[n_in + n_out :]
    chunks = (total_ref[0] + CHUNK - 1) // CHUNK

    def fetch(index):
        slot = lax.rem(index, DEPTH)
        for k in range(CHUNK):
            code = list_ref[index * CHUNK + k]
            pltpu.make_async_copy(
                tiles_hbm.at[lax.shift_right_logical(code, 12)], buf.at[slot, k], sem.at[slot]
            ).start()

    for k in range(DEPTH - 1):

        @pl.when(k < chunks)
        def _():
            fetch(jnp.int32(k))

    per = src_refs[0].shape[0] // EDGE
    for k in range(n_src):
        source[k * per : (k + 1) * per] = src_refs[k][...].reshape(per, EDGE, EDGE)
    source[n_src * per] = jnp.zeros((EDGE, EDGE), BF16)
    acc[...] = jnp.zeros_like(acc)

    def one_chunk(index, carry):
        slot = lax.rem(index, DEPTH)

        @pl.when(index + DEPTH - 1 < chunks)
        def _():
            fetch(index + DEPTH - 1)

        pltpu.make_async_copy(tiles_hbm.at[pl.ds(0, CHUNK)], buf.at[slot], sem.at[slot]).wait()
        for k in range(CHUNK):
            code = list_ref[index * CHUNK + k]
            row_at = lax.shift_right_logical(code, 6) & 63
            col_at = code & 63
            out_at, src_at = (col_at, row_at) if transpose else (row_at, col_at)
            dims = (((0,), (0,)), ((), ())) if transpose else (((1,), (0,)), ((), ()))
            acc[out_at] += lax.dot_general(
                buf[slot, k], source[src_at], dims, preferred_element_type=F32
            )
        return carry

    lax.fori_loop(0, chunks, one_chunk, 0)
    if out_refs[0].dtype == F32:
        out_refs[0][...] = acc[0:HALF_TILES]
        return
    per = out_refs[0].shape[0] // EDGE
    for k in range(n_out):
        total = acc[k * per : (k + 1) * per]
        if has_base:
            total = total + base[k * per : (k + 1) * per]
        out_refs[k][...] = total.reshape(per * EDGE, EDGE).astype(BF16)


def tile_pass(tiles, packed, total, sources, base, out_shape, transpose, name):
    smem = pl.BlockSpec(memory_space=pltpu.SMEM)
    vmem = pl.BlockSpec(memory_space=pltpu.VMEM)
    inputs = list(sources) + ([] if base is None else [base])
    return pl.pallas_call(
        functools.partial(
            tile_kernel, transpose, len(sources), len(out_shape), int(base is not None)
        ),
        out_shape=out_shape,
        in_specs=[smem, smem, pl.BlockSpec(memory_space=pl.ANY)] + [vmem] * len(inputs),
        out_specs=[vmem] * len(out_shape),
        scratch_shapes=[
            pltpu.VMEM((DEPTH, CHUNK, EDGE, EDGE), BF16),
            pltpu.SemaphoreType.DMA((DEPTH,)),
            pltpu.VMEM((HALF_TILES + 1, EDGE, EDGE), BF16),
            pltpu.VMEM((HALF_TILES + 1, EDGE, EDGE), F32),
        ],
        compiler_params=pltpu.CompilerParams(vmem_limit_bytes=VMEM_LIMIT),
        cost_estimate=pl.CostEstimate(
            flops=2 * tiles.size * EDGE, bytes_accessed=2 * tiles.size, transcendentals=0
        ),
        name=name,
    )(total, packed, tiles, *inputs)


def sum_kernel(*refs):
    total = refs[0][...].astype(F32)
    for ref in refs[1:-1]:
        total = total + ref[...].astype(F32)
    refs[-1][...] = total.astype(refs[-1].dtype)


def sum_blocks(blocks, dtype, name):
    vmem = pl.BlockSpec(memory_space=pltpu.VMEM)
    return pl.pallas_call(
        sum_kernel,
        out_shape=jax.ShapeDtypeStruct(blocks[0].shape, dtype),
        in_specs=[vmem] * len(blocks),
        out_specs=vmem,
        compiler_params=pltpu.CompilerParams(vmem_limit_bytes=VMEM_LIMIT),
        name=name,
    )(*blocks)


def sum_pair_kernel(*refs):
    total = refs[0][...].astype(F32)
    for ref in refs[1:-2]:
        total = total + ref[...].astype(F32)
    rows = refs[-1].shape[0]
    refs[-2][...] = total[:rows].astype(refs[-2].dtype)
    refs[-1][...] = total[rows:].astype(refs[-1].dtype)


def sum_pair(blocks, dtypes, name):
    vmem = pl.BlockSpec(memory_space=pltpu.VMEM)
    rows, width = blocks[0].shape
    return pl.pallas_call(
        sum_pair_kernel,
        out_shape=[jax.ShapeDtypeStruct((rows // 2, width), d) for d in dtypes],
        in_specs=[vmem] * len(blocks),
        out_specs=[vmem] * 2,
        compiler_params=pltpu.CompilerParams(vmem_limit_bytes=VMEM_LIMIT),
        name=name,
    )(*blocks)


def middle_kernel(
    scale, feat_ref, own_ref, far_ref, sides_ref, far_sides_ref, bias_ref, far_bias_ref,
    out_ref, hid_ref, gw_ref, agg, w, cot, bias, grad_own,
):
    half = EDGE
    rows = own_ref.shape[0]

    def place(here, there):
        agg[:, here] = own_ref[...]
        agg[:, there] = far_ref[...]
        cot[:, here] = sides_ref[0:rows, :]
        cot[:, there] = far_sides_ref[0:rows, :]
        w[:, here] = sides_ref[rows:, :]
        w[:, there] = far_sides_ref[rows:, :]
        bias[:, here] = bias_ref[...]
        bias[:, there] = far_bias_ref[...]

    left, right = slice(0, half), slice(half, 2 * half)

    @pl.when(feat_ref[0] == 0)
    def _():
        place(left, right)

    @pl.when(feat_ref[0] == 1)
    def _():
        place(right, left)

    lane = pl.multiple_of(feat_ref[0] * half, half)
    pre = jnp.dot(agg[...], w[...], preferred_element_type=F32) + bias[0:1, :]
    sig = jax.nn.sigmoid(pre)
    value = (pre * sig).astype(BF16)
    slope = sig * (1.0 + pre * (1.0 - sig))
    grad = (cot[...].astype(F32) * slope).astype(BF16)

    @pl.when(feat_ref[0] == 0)
    def _():
        out_ref[...] = value[:, left]
        grad_own[...] = grad[:, left]

    @pl.when(feat_ref[0] == 1)
    def _():
        out_ref[...] = value[:, right]
        grad_own[...] = grad[:, right]

    w_rows = w[pl.ds(lane, half), :]
    hid_ref[...] = lax.dot_general(
        grad, w_rows, (((1,), (1,)), ((), ())), preferred_element_type=F32
    ).astype(BF16)
    own = grad_own[...]
    gw_ref[0:256, :] = scale * lax.dot_general(
        agg[...], own, (((0,), (0,)), ((), ())), preferred_element_type=F32
    )
    eighths = jnp.sum(own.astype(F32).reshape(-1, 8, half), axis=0)
    gw_ref[256:264, :] = jnp.broadcast_to(
        scale * jnp.sum(eighths, axis=0, keepdims=True), (8, half)
    )


def middle(scale, feat, own, far, sides, far_sides, bias, far_bias):
    rows = own.shape[0]
    vmem = pl.BlockSpec(memory_space=pltpu.VMEM)
    return pl.pallas_call(
        functools.partial(middle_kernel, scale),
        out_shape=[
            jax.ShapeDtypeStruct((rows, EDGE), BF16),
            jax.ShapeDtypeStruct((rows, EDGE), BF16),
            jax.ShapeDtypeStruct((264, EDGE), F32),
        ],
        in_specs=[pl.BlockSpec(memory_space=pltpu.SMEM)] + [vmem] * 6,
        out_specs=[vmem] * 3,
        scratch_shapes=[
            pltpu.VMEM((rows, 256), BF16),
            pltpu.VMEM((256, 256), BF16),
            pltpu.VMEM((rows, 256), BF16),
            pltpu.VMEM((8, 256), F32),
            pltpu.VMEM((rows, EDGE), BF16),
        ],
        compiler_params=pltpu.CompilerParams(vmem_limit_bytes=VMEM_LIMIT),
        name="middle",
    )(feat, own, far, sides, far_sides, bias, far_bias)


def on_device(tile_vals, tile_rows, tile_cols, tile_count, features, weight, bias_term, cotangent):
    tiles = tile_vals[0, 0]
    rows = tile_rows[0, 0]
    cols = tile_cols[0, 0]
    local_rows = features.shape[0]
    my_zhi, my_x = lax.axis_index("zhi"), lax.axis_index("x")
    my_y, my_zlo = lax.axis_index("y"), lax.axis_index("zlo")
    feat = lax.axis_index("feat").reshape(1)
    node_total = local_rows * 128
    scale = 1.0 / math.sqrt(node_total)

    per = local_rows // EDGE
    row_block, col_block = rows // per, cols // per
    rel_y, rel_zlo = (row_block // 2 - my_y) % 4, (row_block % 2 - my_zlo) % 2
    row_at = (rel_y * 2 + rel_zlo) * per + rows % per
    rel_zhi, rel_x = (col_block // 4 - my_zhi) % 4, (col_block % 4 - my_x) % 4
    second = rel_zhi >= 2
    inner = jnp.where(second, 3 - rel_zhi, rel_zhi)
    col_at = (rel_x * 2 + inner) * per + cols % per
    packed, totals = slot_lists(row_at, col_at, second, tile_count[0, 0])
    lists = [packed[0], packed[1]]
    counts = [totals[0:1], totals[1:2]]

    with jax.named_scope("gather_row"):
        z1, z3, z2 = [pull(features, "zhi", 4, k) for k in (1, 3, 2)]
    with jax.named_scope("sides"):
        sides = jnp.concatenate([cotangent, weight], axis=0)
        bias = jnp.broadcast_to(bias_term[None, :], (8, EDGE))
        far_sides = pull(sides, "feat", 2, 1)
        far_bias = pull(bias, "feat", 2, 1)
    z1, far_sides, far_bias, lists, counts = lax.optimization_barrier(
        (z1, far_sides, far_bias, lists, counts)
    )
    with jax.named_scope("gather_row"):
        near = jnp.concatenate([features, z1], axis=0)
        away = jnp.concatenate([z3, z2], axis=0)
        near_blocks = [near] + [pull(near, "x", 4, k) for k in (1, 2, 3)]
        away_blocks = [away] + [pull(away, "x", 4, k) for k in (1, 2, 3)]

    wide = [jax.ShapeDtypeStruct((HALF_TILES, EDGE, EDGE), F32)]
    block = [jax.ShapeDtypeStruct((local_rows, EDGE), BF16)] * 8
    pair = [jax.ShapeDtypeStruct((2 * local_rows, EDGE), BF16)] * 4
    (base,) = tile_pass(
        tiles, lists[0], counts[0], near_blocks, None, wide, False, "forward_near"
    )
    partial_sums = tile_pass(
        tiles, lists[1], counts[1], away_blocks, base, block, False, "forward_away"
    )

    with jax.named_scope("scatter_col"):
        mine = [partial_sums[0]]
        for k in range(1, 8):
            mine.append(push_col(partial_sums[k], k // 2, k % 2))
    own = sum_blocks(mine, BF16, "sum_col")
    far = pull(own, "feat", 2, 1)
    outputs, hidden, grads = middle(scale, feat, own, far, sides, far_sides, bias, far_bias)

    with jax.named_scope("gather_col"):
        beside = pull(hidden, "zlo", 2, 1)
        blocks = [hidden, beside]
        along = [pull(hidden, "y", 4, k) for k in (1, 2, 3)]
        others = [pull(beside, "y", 4, k) for k in (1, 2, 3)]
        for k in range(3):
            blocks += [along[k], others[k]]
    grads = group_sum(grads, "zlo", 2)
    grads = group_sum(grads, "x", 4)
    back_away = tile_pass(
        tiles, lists[1], counts[1], blocks, None, pair, True, "backward_away"
    )
    with jax.named_scope("scatter_row_away"):
        got = [back_away[0]] + [push(back_away[k], "x", 4, k) for k in (1, 3, 2)]
    near_count, got[1], grads = lax.optimization_barrier((counts[0], got[1], grads))
    grads = group_sum(grads, "zhi", 4)
    back_near = tile_pass(tiles, lists[0], near_count, blocks, None, pair, True, "backward_near")
    *got, back_near = lax.optimization_barrier((*got, back_near))
    z3, z2 = sum_pair(got, (BF16, BF16), "sum_away")
    z2, z3, back_near = lax.optimization_barrier((z2, z3, back_near))
    with jax.named_scope("scatter_row_near"):
        near_got = [back_near[0]] + [push(back_near[k], "x", 4, k) for k in (1, 3, 2)]
    with jax.named_scope("scatter_row_away"):
        z2, z3 = push(z2, "zhi", 4, 2), push(z3, "zhi", 4, 3)
    near_got[1], grads = lax.optimization_barrier((near_got[1], grads))
    grads = group_sum(grads, "y", 4)
    z0, z1 = sum_pair(near_got, (F32, BF16), "sum_near")
    with jax.named_scope("scatter_row_near"):
        z1 = push(z1, "zhi", 4, 1)

    grad_feat = sum_blocks([z0, z1, z2, z3], BF16, "sum_z")
    return outputs, grad_feat, grads[:256], grads[256]


def solution(mesh):
    fine = Mesh(mesh.devices.reshape(4, 4, 4, 2, 2), ("zhi", "x", "y", "zlo", "feat"))
    row, col = ("zhi", "x"), ("y", "zlo")
    nodes = P(row + col, "feat")
    return jax.shard_map(
        on_device,
        mesh=fine,
        in_specs=(
            P(row, col, None, None, None),
            P(row, col, None),
            P(row, col, None),
            P(row, col),
            nodes,
            P(None, "feat"),
            P("feat"),
            nodes,
        ),
        out_specs=(nodes, nodes, P(None, "feat"), P("feat")),
        check_vma=False,
    )
```

```python
import functools
import math

import jax
import jax.numpy as jnp
from jax import lax
from jax.experimental import pallas as pl
from jax.experimental.pallas import tpu as pltpu
from jax.sharding import Mesh
from jax.sharding import PartitionSpec as P

BF16 = jnp.bfloat16
F32 = jnp.float32
EDGE = 128
CHUNK = 32
DEPTH = 3
ROW_TILES = 32
NEAR_TILES = 48
AWAY_TILES = 16
VMEM_LIMIT = 40 * 2**20


def pull(value, axis, size, step):
    return lax.ppermute(value, axis, [((i + step) % size, i) for i in range(size)])


def push(value, axis, size, step):
    return lax.ppermute(value, axis, [(i, (i + step) % size) for i in range(size)])


def push_col(value, step_y, step_z):
    pairs = []
    for y in range(4):
        for z in range(2):
            pairs.append((y * 2 + z, ((y + step_y) % 4) * 2 + (z + step_z) % 2))
    return lax.ppermute(value, ("y", "zlo"), pairs)


def group_sum(value, axis, size):
    with jax.named_scope("weight_grads"):
        parts = [pull(value, axis, size, k) for k in range(1, size)]
        if size == 2:
            return value + parts[0]
        return (value + parts[1]) + (parts[0] + parts[2])


def slot_lists(rows, cols, second, live):
    slots = rows.shape[0]
    index = jnp.arange(slots, dtype=jnp.int32)
    code = index * 4096 + rows * 64 + cols
    kind = jnp.stack([jnp.logical_not(second), second]) & (index < live)[None]
    before = index[None, :] < index[:, None]
    rank = jnp.sum((kind[:, None, :] & before[None]).astype(jnp.int32), axis=2)
    hit = kind[:, None, :] & (rank[:, None, :] == index[None, :, None])
    packed = jnp.sum(jnp.where(hit, code[None, None, :], 0), axis=2)
    totals = jnp.sum(kind.astype(jnp.int32), axis=1)
    spare = 32 * 64 + jnp.array([NEAR_TILES, AWAY_TILES], jnp.int32)
    packed = jnp.where(index[None] < totals[:, None], packed, spare[:, None])
    return packed, totals


def tile_kernel(transpose, n_src, n_out, has_base, total_ref, list_ref, tiles_hbm, *refs):
    src_refs = refs[:n_src]
    base = refs[n_src] if has_base else None
    n_in = n_src + has_base
    out_refs = refs[n_in : n_in + n_out]
    buf, sem, source, acc = refs[n_in + n_out :]
    chunks = (total_ref[0] + CHUNK - 1) // CHUNK

    def fetch(index):
        slot = lax.rem(index, DEPTH)
        for k in range(CHUNK):
            code = list_ref[index * CHUNK + k]
            pltpu.make_async_copy(
                tiles_hbm.at[lax.shift_right_logical(code, 12)], buf.at[slot, k], sem.at[slot]
            ).start()

    for k in range(DEPTH - 1):

        @pl.when(k < chunks)
        def _():
            fetch(jnp.int32(k))

    per = src_refs[0].shape[0] // EDGE
    for k in range(n_src):
        source[k * per : (k + 1) * per] = src_refs[k][...].reshape(per, EDGE, EDGE)
    source[n_src * per :] = jnp.zeros((source.shape[0] - n_src * per, EDGE, EDGE), BF16)
    acc[...] = jnp.zeros_like(acc)

    def one_chunk(index, carry):
        slot = lax.rem(index, DEPTH)

        @pl.when(index + DEPTH - 1 < chunks)
        def _():
            fetch(index + DEPTH - 1)

        pltpu.make_async_copy(tiles_hbm.at[pl.ds(0, CHUNK)], buf.at[slot], sem.at[slot]).wait()
        for k in range(CHUNK):
            code = list_ref[index * CHUNK + k]
            row_at = lax.shift_right_logical(code, 6) & 63
            col_at = code & 63
            out_at, src_at = (col_at, row_at) if transpose else (row_at, col_at)
            dims = (((0,), (0,)), ((), ())) if transpose else (((1,), (0,)), ((), ()))
            acc[out_at] += lax.dot_general(
                buf[slot, k], source[src_at], dims, preferred_element_type=F32
            )
        return carry

    lax.fori_loop(0, chunks, one_chunk, 0)
    if out_refs[0].dtype == F32:
        out_refs[0][...] = acc[0:ROW_TILES]
        return
    per = out_refs[0].shape[0] // EDGE
    for k in range(n_out):
        total = acc[k * per : (k + 1) * per]
        if has_base:
            total = total + base[k * per : (k + 1) * per]
        out_refs[k][...] = total.reshape(per * EDGE, EDGE).astype(BF16)


def tile_pass(tiles, packed, total, sources, base, out_shape, transpose, name):
    smem = pl.BlockSpec(memory_space=pltpu.SMEM)
    vmem = pl.BlockSpec(memory_space=pltpu.VMEM)
    inputs = list(sources) + ([] if base is None else [base])
    out_tiles = sum(math.prod(shape.shape) for shape in out_shape) // (EDGE * EDGE)
    return pl.pallas_call(
        functools.partial(
            tile_kernel, transpose, len(sources), len(out_shape), int(base is not None)
        ),
        out_shape=out_shape,
        in_specs=[smem, smem, pl.BlockSpec(memory_space=pl.ANY)] + [vmem] * len(inputs),
        out_specs=[vmem] * len(out_shape),
        scratch_shapes=[
            pltpu.VMEM((DEPTH, CHUNK, EDGE, EDGE), BF16),
            pltpu.SemaphoreType.DMA((DEPTH,)),
            pltpu.VMEM((NEAR_TILES + 1, EDGE, EDGE), BF16),
            pltpu.VMEM((out_tiles + 1, EDGE, EDGE), F32),
        ],
        compiler_params=pltpu.CompilerParams(vmem_limit_bytes=VMEM_LIMIT),
        cost_estimate=pl.CostEstimate(
            flops=2 * tiles.size * EDGE, bytes_accessed=2 * tiles.size, transcendentals=0
        ),
        name=name,
    )(total, packed, tiles, *inputs)


def sum_kernel(*refs):
    total = refs[0][...].astype(F32)
    for ref in refs[1:-1]:
        total = total + ref[...].astype(F32)
    refs[-1][...] = total.astype(refs[-1].dtype)


def sum_blocks(blocks, dtype, name):
    vmem = pl.BlockSpec(memory_space=pltpu.VMEM)
    return pl.pallas_call(
        sum_kernel,
        out_shape=jax.ShapeDtypeStruct(blocks[0].shape, dtype),
        in_specs=[vmem] * len(blocks),
        out_specs=vmem,
        compiler_params=pltpu.CompilerParams(vmem_limit_bytes=VMEM_LIMIT),
        name=name,
    )(*blocks)


def split_sum_kernel(n, *refs):
    rows = refs[n].shape[0]
    for k, out in enumerate(refs[n:]):
        total = refs[0][k * rows : (k + 1) * rows, :].astype(F32)
        for ref in refs[1:n]:
            total = total + ref[k * rows : (k + 1) * rows, :].astype(F32)
        out[...] = total.astype(out.dtype)


def split_sum(blocks, dtypes, name):
    vmem = pl.BlockSpec(memory_space=pltpu.VMEM)
    rows, width = blocks[0].shape
    return pl.pallas_call(
        functools.partial(split_sum_kernel, len(blocks)),
        out_shape=[jax.ShapeDtypeStruct((rows // len(dtypes), width), d) for d in dtypes],
        in_specs=[vmem] * len(blocks),
        out_specs=[vmem] * len(dtypes),
        compiler_params=pltpu.CompilerParams(vmem_limit_bytes=VMEM_LIMIT),
        name=name,
    )(*blocks)


def middle_kernel(
    scale, feat_ref, own_ref, far_ref, sides_ref, far_sides_ref, bias_ref, far_bias_ref,
    out_ref, hid_ref, gw_ref, agg, w, cot, bias, grad_own,
):
    half = EDGE
    rows = own_ref.shape[0]

    def place(here, there):
        agg[:, here] = own_ref[...]
        agg[:, there] = far_ref[...]
        cot[:, here] = sides_ref[0:rows, :]
        cot[:, there] = far_sides_ref[0:rows, :]
        w[:, here] = sides_ref[rows:, :]
        w[:, there] = far_sides_ref[rows:, :]
        bias[:, here] = bias_ref[...]
        bias[:, there] = far_bias_ref[...]

    left, right = slice(0, half), slice(half, 2 * half)

    @pl.when(feat_ref[0] == 0)
    def _():
        place(left, right)

    @pl.when(feat_ref[0] == 1)
    def _():
        place(right, left)

    lane = pl.multiple_of(feat_ref[0] * half, half)
    pre = jnp.dot(agg[...], w[...], preferred_element_type=F32) + bias[0:1, :]
    sig = jax.nn.sigmoid(pre)
    value = (pre * sig).astype(BF16)
    slope = sig * (1.0 + pre * (1.0 - sig))
    grad = (cot[...].astype(F32) * slope).astype(BF16)

    @pl.when(feat_ref[0] == 0)
    def _():
        out_ref[...] = value[:, left]
        grad_own[...] = grad[:, left]

    @pl.when(feat_ref[0] == 1)
    def _():
        out_ref[...] = value[:, right]
        grad_own[...] = grad[:, right]

    w_rows = w[pl.ds(lane, half), :]
    hid_ref[...] = lax.dot_general(
        grad, w_rows, (((1,), (1,)), ((), ())), preferred_element_type=F32
    ).astype(BF16)
    own = grad_own[...]
    gw_ref[0:256, :] = scale * lax.dot_general(
        agg[...], own, (((0,), (0,)), ((), ())), preferred_element_type=F32
    )
    eighths = jnp.sum(own.astype(F32).reshape(-1, 8, half), axis=0)
    gw_ref[256:264, :] = jnp.broadcast_to(
        scale * jnp.sum(eighths, axis=0, keepdims=True), (8, half)
    )


def middle(scale, feat, own, far, sides, far_sides, bias, far_bias):
    rows = own.shape[0]
    vmem = pl.BlockSpec(memory_space=pltpu.VMEM)
    return pl.pallas_call(
        functools.partial(middle_kernel, scale),
        out_shape=[
            jax.ShapeDtypeStruct((rows, EDGE), BF16),
            jax.ShapeDtypeStruct((rows, EDGE), BF16),
            jax.ShapeDtypeStruct((264, EDGE), F32),
        ],
        in_specs=[pl.BlockSpec(memory_space=pltpu.SMEM)] + [vmem] * 6,
        out_specs=[vmem] * 3,
        scratch_shapes=[
            pltpu.VMEM((rows, 256), BF16),
            pltpu.VMEM((256, 256), BF16),
            pltpu.VMEM((rows, 256), BF16),
            pltpu.VMEM((8, 256), F32),
            pltpu.VMEM((rows, EDGE), BF16),
        ],
        compiler_params=pltpu.CompilerParams(vmem_limit_bytes=VMEM_LIMIT),
        name="middle",
    )(feat, own, far, sides, far_sides, bias, far_bias)


def on_device(tile_vals, tile_rows, tile_cols, tile_count, features, weight, bias_term, cotangent):
    tiles = tile_vals[0, 0]
    rows = tile_rows[0, 0]
    cols = tile_cols[0, 0]
    local_rows = features.shape[0]
    my_zhi, my_x = lax.axis_index("zhi"), lax.axis_index("x")
    my_y, my_zlo = lax.axis_index("y"), lax.axis_index("zlo")
    feat = lax.axis_index("feat").reshape(1)
    node_total = local_rows * 128
    scale = 1.0 / math.sqrt(node_total)

    per = local_rows // EDGE
    row_block, col_block = rows // per, cols // per
    rel_y, rel_zlo = (row_block // 2 - my_y) % 4, (row_block % 2 - my_zlo) % 2
    row_at = (rel_y * 2 + rel_zlo) * per + rows % per
    rel_zhi, rel_x = (col_block // 4 - my_zhi) % 4, (col_block % 4 - my_x) % 4
    second = rel_x == 2
    turn = jnp.where(second, 0, (rel_x + 1) // 2)
    col_at = (turn * 4 + rel_zhi) * per + cols % per
    packed, totals = slot_lists(row_at, col_at, second, tile_count[0, 0])
    lists = [packed[0], packed[1]]
    counts = [totals[0:1], totals[1:2]]

    with jax.named_scope("gather_row"):
        z2, z1, z3 = [pull(features, "zhi", 4, k) for k in (2, 1, 3)]
    with jax.named_scope("sides"):
        sides = jnp.concatenate([cotangent, weight], axis=0)
        bias = jnp.broadcast_to(bias_term[None, :], (8, EDGE))
        far_sides = pull(sides, "feat", 2, 1)
        far_bias = pull(bias, "feat", 2, 1)
    z1, z2, z3, far_sides, far_bias, lists, counts = lax.optimization_barrier(
        (z1, z2, z3, far_sides, far_bias, lists, counts)
    )
    with jax.named_scope("gather_row"):
        line = jnp.concatenate([features, z1, z2, z3], axis=0)
        x1, x3, x2 = [pull(line, "x", 4, k) for k in (1, 3, 2)]

    wide = [jax.ShapeDtypeStruct((ROW_TILES, EDGE, EDGE), F32)]
    block = jax.ShapeDtypeStruct((local_rows, EDGE), BF16)
    whole = jax.ShapeDtypeStruct((4 * local_rows, EDGE), BF16)
    (base,) = tile_pass(
        tiles, lists[0], counts[0], [line, x1, x3], None, wide, False, "forward_near"
    )
    partial_sums = tile_pass(
        tiles, lists[1], counts[1], [x2], base, [block] * 8, False, "forward_away"
    )

    with jax.named_scope("scatter_col"):
        mine = [partial_sums[0]]
        for k in range(1, 8):
            mine.append(push_col(partial_sums[k], k // 2, k % 2))
    own = sum_blocks(mine, BF16, "sum_col")
    far = pull(own, "feat", 2, 1)
    outputs, hidden, grads = middle(scale, feat, own, far, sides, far_sides, bias, far_bias)

    with jax.named_scope("gather_col"):
        beside = pull(hidden, "zlo", 2, 1)
        blocks = [hidden, beside]
        along = [pull(hidden, "y", 4, k) for k in (1, 2, 3)]
        others = [pull(beside, "y", 4, k) for k in (1, 2, 3)]
        for k in range(3):
            blocks += [along[k], others[k]]
    grads = group_sum(grads, "zlo", 2)
    grads = group_sum(grads, "x", 4)
    (back_away,) = tile_pass(
        tiles, lists[1], counts[1], blocks, None, [whole], True, "backward_away"
    )
    back_away, grads = lax.optimization_barrier((back_away, grads))
    with jax.named_scope("scatter_row"):
        x2 = push(back_away, "x", 4, 2)
    grads = group_sum(grads, "zhi", 4)
    near_count, grads = lax.optimization_barrier((counts[0], grads))
    back_near = tile_pass(
        tiles, lists[0], near_count, blocks, None, [whole] * 3, True, "backward_near"
    )
    back_near, grads = lax.optimization_barrier((back_near, grads))
    with jax.named_scope("scatter_row"):
        x1, x3 = push(back_near[1], "x", 4, 1), push(back_near[2], "x", 4, 3)
        sums = split_sum([back_near[0], x1, x3, x2], (F32, BF16, BF16, BF16), "sum_x")
        along_z = [push(sums[k], "zhi", 4, k) for k in (2, 1, 3)]
    grads = group_sum(grads, "y", 4)
    grad_feat = sum_blocks([sums[0]] + along_z, BF16, "sum_z")
    return outputs, grad_feat, grads[:256], grads[256]


def solution(mesh):
    fine = Mesh(mesh.devices.reshape(4, 4, 4, 2, 2), ("zhi", "x", "y", "zlo", "feat"))
    row, col = ("zhi", "x"), ("y", "zlo")
    nodes = P(row + col, "feat")
    return jax.shard_map(
        on_device,
        mesh=fine,
        in_specs=(
            P(row, col, None, None, None),
            P(row, col, None),
            P(row, col, None),
            P(row, col),
            nodes,
            P(None, "feat"),
            P("feat"),
            nodes,
        ),
        out_specs=(nodes, nodes, P(None, "feat"), P("feat")),
        check_vma=False,
    )
```

```python
import functools
import math

import jax
import jax.numpy as jnp
from jax import lax
from jax.experimental import pallas as pl
from jax.experimental.pallas import tpu as pltpu
from jax.sharding import Mesh
from jax.sharding import PartitionSpec as P

BF16 = jnp.bfloat16
F32 = jnp.float32
EDGE = 128
CHUNK = 32
DEPTH = 3
HALF_TILES = 32
VMEM_LIMIT = 40 * 2**20


def pull(value, axis, size, step):
    return lax.ppermute(value, axis, [((i + step) % size, i) for i in range(size)])


def push(value, axis, size, step):
    return lax.ppermute(value, axis, [(i, (i + step) % size) for i in range(size)])


def push_col(value, step_y, step_z):
    pairs = []
    for y in range(4):
        for z in range(2):
            pairs.append((y * 2 + z, ((y + step_y) % 4) * 2 + (z + step_z) % 2))
    return lax.ppermute(value, ("y", "zlo"), pairs)


def slot_lists(rows, cols, second, live):
    slots = rows.shape[0]
    index = jnp.arange(slots, dtype=jnp.int32)
    code = index * 4096 + rows * 64 + cols
    kind = jnp.stack([jnp.logical_not(second), second]) & (index < live)[None]
    before = index[None, :] < index[:, None]
    rank = jnp.sum((kind[:, None, :] & before[None]).astype(jnp.int32), axis=2)
    hit = kind[:, None, :] & (rank[:, None, :] == index[None, :, None])
    packed = jnp.sum(jnp.where(hit, code[None, None, :], 0), axis=2)
    totals = jnp.sum(kind.astype(jnp.int32), axis=1)
    packed = jnp.where(index[None] < totals[:, None], packed, 32 * 64 + 32)
    return packed, totals


def tile_kernel(transpose, n_src, n_out, has_base, total_ref, list_ref, tiles_hbm, *refs):
    src_refs = refs[:n_src]
    base = refs[n_src] if has_base else None
    n_in = n_src + has_base
    out_refs = refs[n_in : n_in + n_out]
    buf, sem, source, acc = refs[n_in + n_out :]
    chunks = (total_ref[0] + CHUNK - 1) // CHUNK

    def fetch(index):
        slot = lax.rem(index, DEPTH)
        for k in range(CHUNK):
            code = list_ref[index * CHUNK + k]
            pltpu.make_async_copy(
                tiles_hbm.at[lax.shift_right_logical(code, 12)], buf.at[slot, k], sem.at[slot]
            ).start()

    for k in range(DEPTH - 1):

        @pl.when(k < chunks)
        def _():
            fetch(jnp.int32(k))

    per = src_refs[0].shape[0] // EDGE
    for k in range(n_src):
        source[k * per : (k + 1) * per] = src_refs[k][...].reshape(per, EDGE, EDGE)
    source[n_src * per] = jnp.zeros((EDGE, EDGE), BF16)
    acc[...] = jnp.zeros_like(acc)

    def one_chunk(index, carry):
        slot = lax.rem(index, DEPTH)

        @pl.when(index + DEPTH - 1 < chunks)
        def _():
            fetch(index + DEPTH - 1)

        pltpu.make_async_copy(tiles_hbm.at[pl.ds(0, CHUNK)], buf.at[slot], sem.at[slot]).wait()
        for k in range(CHUNK):
            code = list_ref[index * CHUNK + k]
            row_at = lax.shift_right_logical(code, 6) & 63
            col_at = code & 63
            out_at, src_at = (col_at, row_at) if transpose else (row_at, col_at)
            dims = (((0,), (0,)), ((), ())) if transpose else (((1,), (0,)), ((), ()))
            acc[out_at] += lax.dot_general(
                buf[slot, k], source[src_at], dims, preferred_element_type=F32
            )
        return carry

    lax.fori_loop(0, chunks, one_chunk, 0)
    if out_refs[0].dtype == F32:
        out_refs[0][...] = acc[0:HALF_TILES]
        return
    per = out_refs[0].shape[0] // EDGE
    for k in range(n_out):
        total = acc[k * per : (k + 1) * per]
        if has_base:
            total = total + base[k * per : (k + 1) * per]
        out_refs[k][...] = total.reshape(per * EDGE, EDGE).astype(BF16)


def tile_pass(tiles, packed, total, sources, base, out_shape, transpose, name):
    smem = pl.BlockSpec(memory_space=pltpu.SMEM)
    vmem = pl.BlockSpec(memory_space=pltpu.VMEM)
    inputs = list(sources) + ([] if base is None else [base])
    return pl.pallas_call(
        functools.partial(
            tile_kernel, transpose, len(sources), len(out_shape), int(base is not None)
        ),
        out_shape=out_shape,
        in_specs=[smem, smem, pl.BlockSpec(memory_space=pl.ANY)] + [vmem] * len(inputs),
        out_specs=[vmem] * len(out_shape),
        scratch_shapes=[
            pltpu.VMEM((DEPTH, CHUNK, EDGE, EDGE), BF16),
            pltpu.SemaphoreType.DMA((DEPTH,)),
            pltpu.VMEM((HALF_TILES + 1, EDGE, EDGE), BF16),
            pltpu.VMEM((HALF_TILES + 1, EDGE, EDGE), F32),
        ],
        compiler_params=pltpu.CompilerParams(vmem_limit_bytes=VMEM_LIMIT),
        cost_estimate=pl.CostEstimate(
            flops=2 * tiles.size * EDGE, bytes_accessed=2 * tiles.size, transcendentals=0
        ),
        name=name,
    )(total, packed, tiles, *inputs)


def sum_kernel(*refs):
    total = refs[0][...].astype(F32)
    for ref in refs[1:-1]:
        total = total + ref[...].astype(F32)
    refs[-1][...] = total.astype(refs[-1].dtype)


def sum_blocks(blocks, dtype, name):
    vmem = pl.BlockSpec(memory_space=pltpu.VMEM)
    return pl.pallas_call(
        sum_kernel,
        out_shape=jax.ShapeDtypeStruct(blocks[0].shape, dtype),
        in_specs=[vmem] * len(blocks),
        out_specs=vmem,
        compiler_params=pltpu.CompilerParams(vmem_limit_bytes=VMEM_LIMIT),
        name=name,
    )(*blocks)


def sum_pair_kernel(*refs):
    total = refs[0][...].astype(F32)
    for ref in refs[1:-2]:
        total = total + ref[...].astype(F32)
    rows = refs[-1].shape[0]
    refs[-2][...] = total[:rows].astype(refs[-2].dtype)
    refs[-1][...] = total[rows:].astype(refs[-1].dtype)


def sum_pair(blocks, dtypes, name):
    vmem = pl.BlockSpec(memory_space=pltpu.VMEM)
    rows, width = blocks[0].shape
    return pl.pallas_call(
        sum_pair_kernel,
        out_shape=[jax.ShapeDtypeStruct((rows // 2, width), d) for d in dtypes],
        in_specs=[vmem] * len(blocks),
        out_specs=[vmem] * 2,
        compiler_params=pltpu.CompilerParams(vmem_limit_bytes=VMEM_LIMIT),
        name=name,
    )(*blocks)


def middle_kernel(
    scale, feat_ref, own_ref, far_ref, sides_ref, far_sides_ref, bias_ref, far_bias_ref,
    out_ref, hid_ref, gw_ref, agg, w, cot, bias, grad_own,
):
    half = EDGE
    rows = own_ref.shape[0]

    def place(here, there):
        agg[:, here] = own_ref[...]
        agg[:, there] = far_ref[...]
        cot[:, here] = sides_ref[0:rows, :]
        cot[:, there] = far_sides_ref[0:rows, :]
        w[:, here] = sides_ref[rows:, :]
        w[:, there] = far_sides_ref[rows:, :]
        bias[:, here] = bias_ref[...]
        bias[:, there] = far_bias_ref[...]

    left, right = slice(0, half), slice(half, 2 * half)

    @pl.when(feat_ref[0] == 0)
    def _():
        place(left, right)

    @pl.when(feat_ref[0] == 1)
    def _():
        place(right, left)

    lane = pl.multiple_of(feat_ref[0] * half, half)
    pre = jnp.dot(agg[...], w[...], preferred_element_type=F32) + bias[0:1, :]
    sig = jax.nn.sigmoid(pre)
    value = (pre * sig).astype(BF16)
    slope = sig * (1.0 + pre * (1.0 - sig))
    grad = (cot[...].astype(F32) * slope).astype(BF16)

    @pl.when(feat_ref[0] == 0)
    def _():
        out_ref[...] = value[:, left]
        grad_own[...] = grad[:, left]

    @pl.when(feat_ref[0] == 1)
    def _():
        out_ref[...] = value[:, right]
        grad_own[...] = grad[:, right]

    w_rows = w[pl.ds(lane, half), :]
    hid_ref[...] = lax.dot_general(
        grad, w_rows, (((1,), (1,)), ((), ())), preferred_element_type=F32
    ).astype(BF16)
    own = grad_own[...]
    gw_ref[0:256, :] = scale * lax.dot_general(
        agg[...], own, (((0,), (0,)), ((), ())), preferred_element_type=F32
    )
    eighths = jnp.sum(own.astype(F32).reshape(-1, 8, half), axis=0)
    gw_ref[256:264, :] = jnp.broadcast_to(
        scale * jnp.sum(eighths, axis=0, keepdims=True), (8, half)
    )


def middle(scale, feat, own, far, sides, far_sides, bias, far_bias):
    rows = own.shape[0]
    vmem = pl.BlockSpec(memory_space=pltpu.VMEM)
    return pl.pallas_call(
        functools.partial(middle_kernel, scale),
        out_shape=[
            jax.ShapeDtypeStruct((rows, EDGE), BF16),
            jax.ShapeDtypeStruct((rows, EDGE), BF16),
            jax.ShapeDtypeStruct((264, EDGE), F32),
        ],
        in_specs=[pl.BlockSpec(memory_space=pltpu.SMEM)] + [vmem] * 6,
        out_specs=[vmem] * 3,
        scratch_shapes=[
            pltpu.VMEM((rows, 256), BF16),
            pltpu.VMEM((256, 256), BF16),
            pltpu.VMEM((rows, 256), BF16),
            pltpu.VMEM((8, 256), F32),
            pltpu.VMEM((rows, EDGE), BF16),
        ],
        compiler_params=pltpu.CompilerParams(vmem_limit_bytes=VMEM_LIMIT),
        name="middle",
    )(feat, own, far, sides, far_sides, bias, far_bias)


def on_device(tile_vals, tile_rows, tile_cols, tile_count, features, weight, bias_term, cotangent):
    tiles = tile_vals[0, 0]
    rows = tile_rows[0, 0]
    cols = tile_cols[0, 0]
    local_rows = features.shape[0]
    my_zhi, my_x = lax.axis_index("zhi"), lax.axis_index("x")
    my_y, my_zlo = lax.axis_index("y"), lax.axis_index("zlo")
    feat = lax.axis_index("feat").reshape(1)
    node_total = local_rows * 128
    scale = 1.0 / math.sqrt(node_total)

    with jax.named_scope("gather_row"):
        z2, z1, z3 = [pull(features, "zhi", 4, k) for k in (2, 1, 3)]
    with jax.named_scope("sides"):
        sides = jnp.concatenate([cotangent, weight], axis=0)
        bias = jnp.broadcast_to(bias_term[None, :], (8, EDGE))
        far_sides = pull(sides, "feat", 2, 1)
        far_bias = pull(bias, "feat", 2, 1)
    z1, z2, z3, far_sides, far_bias = lax.optimization_barrier(
        (z1, z2, z3, far_sides, far_bias)
    )
    with jax.named_scope("gather_row"):
        near = jnp.concatenate([features, z1], axis=0)
        away = jnp.concatenate([z3, z2], axis=0)
        near_blocks = [near] + [pull(near, "x", 4, k) for k in (1, 2, 3)]
        away_blocks = [away] + [pull(away, "x", 4, k) for k in (1, 2, 3)]
    near_blocks[0], rows, cols = lax.optimization_barrier((near, rows, cols))

    per = local_rows // EDGE
    row_block, col_block = rows // per, cols // per
    rel_y, rel_zlo = (row_block // 2 - my_y) % 4, (row_block % 2 - my_zlo) % 2
    row_at = (rel_y * 2 + rel_zlo) * per + rows % per
    rel_zhi, rel_x = (col_block // 4 - my_zhi) % 4, (col_block % 4 - my_x) % 4
    second = rel_zhi >= 2
    inner = jnp.where(second, 3 - rel_zhi, rel_zhi)
    col_at = (rel_x * 2 + inner) * per + cols % per
    packed, totals = slot_lists(row_at, col_at, second, tile_count[0, 0])
    lists = [packed[0], packed[1]]
    counts = [totals[0:1], totals[1:2]]

    wide = [jax.ShapeDtypeStruct((HALF_TILES, EDGE, EDGE), F32)]
    block = [jax.ShapeDtypeStruct((local_rows, EDGE), BF16)] * 8
    pair = [jax.ShapeDtypeStruct((2 * local_rows, EDGE), BF16)] * 4
    (base,) = tile_pass(
        tiles, lists[0], counts[0], near_blocks, None, wide, False, "forward_near"
    )
    partial_sums = tile_pass(
        tiles, lists[1], counts[1], away_blocks, base, block, False, "forward_away"
    )

    with jax.named_scope("scatter_col"):
        mine = [partial_sums[0]]
        for k in range(1, 8):
            mine.append(push_col(partial_sums[k], k // 2, k % 2))
    own = sum_blocks(mine, BF16, "sum_col")
    far = pull(own, "feat", 2, 1)
    outputs, hidden, grads = middle(scale, feat, own, far, sides, far_sides, bias, far_bias)

    with jax.named_scope("gather_col"):
        beside = pull(hidden, "zlo", 2, 1)
        blocks = [hidden, beside]
        along = [pull(hidden, "y", 4, k) for k in (1, 2, 3)]
        others = [pull(beside, "y", 4, k) for k in (1, 2, 3)]
        for k in range(3):
            blocks += [along[k], others[k]]
    with jax.named_scope("weight_grads"):
        grads = grads + pull(grads, "zlo", 2, 1)
        grads = lax.psum(grads, "x")
    back_away = tile_pass(
        tiles, lists[1], counts[1], blocks, None, pair, True, "backward_away"
    )
    back_away, grads = lax.optimization_barrier((back_away, grads))
    with jax.named_scope("weight_grads"):
        grads = lax.psum(grads, "y")
    with jax.named_scope("scatter_row_away"):
        got = [back_away[0]] + [push(back_away[k], "x", 4, k) for k in (1, 3, 2)]
    near_count, got[1] = lax.optimization_barrier((counts[0], got[1]))
    back_near = tile_pass(tiles, lists[0], near_count, blocks, None, pair, True, "backward_near")
    *got, back_near = lax.optimization_barrier((*got, back_near))
    z3, z2 = sum_pair(got, (BF16, BF16), "sum_away")
    z2, z3, back_near, grads = lax.optimization_barrier((z2, z3, back_near, grads))
    with jax.named_scope("weight_grads"):
        grads = lax.psum(grads, "zhi")
    with jax.named_scope("scatter_row_near"):
        near_got = [back_near[0]] + [push(back_near[k], "x", 4, k) for k in (1, 3, 2)]
    with jax.named_scope("scatter_row_away"):
        z2, z3 = push(z2, "zhi", 4, 2), push(z3, "zhi", 4, 3)
    z0, z1 = sum_pair(near_got, (F32, BF16), "sum_near")
    with jax.named_scope("scatter_row_near"):
        z1 = push(z1, "zhi", 4, 1)

    grad_feat = sum_blocks([z0, z1, z2, z3], BF16, "sum_z")
    return outputs, grad_feat, grads[:256], grads[256]


def solution(mesh):
    fine = Mesh(mesh.devices.reshape(4, 4, 4, 2, 2), ("zhi", "x", "y", "zlo", "feat"))
    row, col = ("zhi", "x"), ("y", "zlo")
    nodes = P(row + col, "feat")
    return jax.shard_map(
        on_device,
        mesh=fine,
        in_specs=(
            P(row, col, None, None, None),
            P(row, col, None),
            P(row, col, None),
            P(row, col),
            nodes,
            P(None, "feat"),
            P("feat"),
            nodes,
        ),
        out_specs=(nodes, nodes, P(None, "feat"), P("feat")),
        check_vma=False,
    )
```

```python
import functools
import math

import jax
import jax.numpy as jnp
from jax import lax
from jax.experimental import pallas as pl
from jax.experimental.pallas import tpu as pltpu
from jax.sharding import Mesh
from jax.sharding import PartitionSpec as P

BF16 = jnp.bfloat16
F32 = jnp.float32
EDGE = 128
CHUNK = 32
DEPTH = 3
HALF_TILES = 32
VMEM_LIMIT = 40 * 2**20


def pull(value, axis, size, step):
    return lax.ppermute(value, axis, [((i + step) % size, i) for i in range(size)])


def push(value, axis, size, step):
    return lax.ppermute(value, axis, [(i, (i + step) % size) for i in range(size)])


def push_col(value, step_y, step_z):
    pairs = []
    for y in range(4):
        for z in range(2):
            pairs.append((y * 2 + z, ((y + step_y) % 4) * 2 + (z + step_z) % 2))
    return lax.ppermute(value, ("y", "zlo"), pairs)


def pair_sum(value, axis, size, flip):
    with jax.named_scope("weight_grads"):
        return value + lax.ppermute(value, axis, [(i, i ^ flip) for i in range(size)])


def slot_lists(rows, cols, second, live):
    slots = rows.shape[0]
    index = jnp.arange(slots, dtype=jnp.int32)
    code = index * 4096 + rows * 64 + cols
    kind = jnp.stack([jnp.logical_not(second), second]) & (index < live)[None]
    before = index[None, :] < index[:, None]
    rank = jnp.sum((kind[:, None, :] & before[None]).astype(jnp.int32), axis=2)
    hit = kind[:, None, :] & (rank[:, None, :] == index[None, :, None])
    packed = jnp.sum(jnp.where(hit, code[None, None, :], 0), axis=2)
    totals = jnp.sum(kind.astype(jnp.int32), axis=1)
    packed = jnp.where(index[None] < totals[:, None], packed, 32 * 64 + 32)
    return packed, totals


def tile_kernel(transpose, n_src, n_out, has_base, total_ref, list_ref, tiles_hbm, *refs):
    src_refs = refs[:n_src]
    base = refs[n_src] if has_base else None
    n_in = n_src + has_base
    out_refs = refs[n_in : n_in + n_out]
    buf, sem, source, acc = refs[n_in + n_out :]
    chunks = (total_ref[0] + CHUNK - 1) // CHUNK

    def fetch(index):
        slot = lax.rem(index, DEPTH)
        for k in range(CHUNK):
            code = list_ref[index * CHUNK + k]
            pltpu.make_async_copy(
                tiles_hbm.at[lax.shift_right_logical(code, 12)], buf.at[slot, k], sem.at[slot]
            ).start()

    for k in range(DEPTH - 1):

        @pl.when(k < chunks)
        def _():
            fetch(jnp.int32(k))

    per = src_refs[0].shape[0] // EDGE
    for k in range(n_src):
        source[k * per : (k + 1) * per] = src_refs[k][...].reshape(per, EDGE, EDGE)
    source[n_src * per] = jnp.zeros((EDGE, EDGE), BF16)
    acc[...] = jnp.zeros_like(acc)

    def one_chunk(index, carry):
        slot = lax.rem(index, DEPTH)

        @pl.when(index + DEPTH - 1 < chunks)
        def _():
            fetch(index + DEPTH - 1)

        pltpu.make_async_copy(tiles_hbm.at[pl.ds(0, CHUNK)], buf.at[slot], sem.at[slot]).wait()
        for k in range(CHUNK):
            code = list_ref[index * CHUNK + k]
            row_at = lax.shift_right_logical(code, 6) & 63
            col_at = code & 63
            out_at, src_at = (col_at, row_at) if transpose else (row_at, col_at)
            dims = (((0,), (0,)), ((), ())) if transpose else (((1,), (0,)), ((), ()))
            acc[out_at] += lax.dot_general(
                buf[slot, k], source[src_at], dims, preferred_element_type=F32
            )
        return carry

    lax.fori_loop(0, chunks, one_chunk, 0)
    if out_refs[0].dtype == F32:
        out_refs[0][...] = acc[0:HALF_TILES]
        return
    per = out_refs[0].shape[0] // EDGE
    for k in range(n_out):
        total = acc[k * per : (k + 1) * per]
        if has_base:
            total = total + base[k * per : (k + 1) * per]
        out_refs[k][...] = total.reshape(per * EDGE, EDGE).astype(BF16)


def tile_pass(tiles, packed, total, sources, base, out_shape, transpose, name):
    smem = pl.BlockSpec(memory_space=pltpu.SMEM)
    vmem = pl.BlockSpec(memory_space=pltpu.VMEM)
    inputs = list(sources) + ([] if base is None else [base])
    return pl.pallas_call(
        functools.partial(
            tile_kernel, transpose, len(sources), len(out_shape), int(base is not None)
        ),
        out_shape=out_shape,
        in_specs=[smem, smem, pl.BlockSpec(memory_space=pl.ANY)] + [vmem] * len(inputs),
        out_specs=[vmem] * len(out_shape),
        scratch_shapes=[
            pltpu.VMEM((DEPTH, CHUNK, EDGE, EDGE), BF16),
            pltpu.SemaphoreType.DMA((DEPTH,)),
            pltpu.VMEM((HALF_TILES + 1, EDGE, EDGE), BF16),
            pltpu.VMEM((HALF_TILES + 1, EDGE, EDGE), F32),
        ],
        compiler_params=pltpu.CompilerParams(vmem_limit_bytes=VMEM_LIMIT),
        cost_estimate=pl.CostEstimate(
            flops=2 * tiles.size * EDGE, bytes_accessed=2 * tiles.size, transcendentals=0
        ),
        name=name,
    )(total, packed, tiles, *inputs)


def sum_kernel(*refs):
    total = refs[0][...].astype(F32)
    for ref in refs[1:-1]:
        total = total + ref[...].astype(F32)
    refs[-1][...] = total.astype(refs[-1].dtype)


def sum_blocks(blocks, dtype, name):
    vmem = pl.BlockSpec(memory_space=pltpu.VMEM)
    return pl.pallas_call(
        sum_kernel,
        out_shape=jax.ShapeDtypeStruct(blocks[0].shape, dtype),
        in_specs=[vmem] * len(blocks),
        out_specs=vmem,
        compiler_params=pltpu.CompilerParams(vmem_limit_bytes=VMEM_LIMIT),
        name=name,
    )(*blocks)


def sum_pair_kernel(*refs):
    total = refs[0][...].astype(F32)
    for ref in refs[1:-2]:
        total = total + ref[...].astype(F32)
    rows = refs[-1].shape[0]
    refs[-2][...] = total[:rows].astype(refs[-2].dtype)
    refs[-1][...] = total[rows:].astype(refs[-1].dtype)


def sum_pair(blocks, dtypes, name):
    vmem = pl.BlockSpec(memory_space=pltpu.VMEM)
    rows, width = blocks[0].shape
    return pl.pallas_call(
        sum_pair_kernel,
        out_shape=[jax.ShapeDtypeStruct((rows // 2, width), d) for d in dtypes],
        in_specs=[vmem] * len(blocks),
        out_specs=[vmem] * 2,
        compiler_params=pltpu.CompilerParams(vmem_limit_bytes=VMEM_LIMIT),
        name=name,
    )(*blocks)


def middle_kernel(
    scale, feat_ref, own_ref, far_ref, sides_ref, far_sides_ref, bias_ref, far_bias_ref,
    out_ref, hid_ref, gw_ref, agg, w, cot, bias, grad_own,
):
    half = EDGE
    rows = own_ref.shape[0]

    def place(here, there):
        agg[:, here] = own_ref[...]
        agg[:, there] = far_ref[...]
        cot[:, here] = sides_ref[0:rows, :]
        cot[:, there] = far_sides_ref[0:rows, :]
        w[:, here] = sides_ref[rows:, :]
        w[:, there] = far_sides_ref[rows:, :]
        bias[:, here] = bias_ref[...]
        bias[:, there] = far_bias_ref[...]

    left, right = slice(0, half), slice(half, 2 * half)

    @pl.when(feat_ref[0] == 0)
    def _():
        place(left, right)

    @pl.when(feat_ref[0] == 1)
    def _():
        place(right, left)

    lane = pl.multiple_of(feat_ref[0] * half, half)
    pre = jnp.dot(agg[...], w[...], preferred_element_type=F32) + bias[0:1, :]
    sig = jax.nn.sigmoid(pre)
    value = (pre * sig).astype(BF16)
    slope = sig * (1.0 + pre * (1.0 - sig))
    grad = (cot[...].astype(F32) * slope).astype(BF16)

    @pl.when(feat_ref[0] == 0)
    def _():
        out_ref[...] = value[:, left]
        grad_own[...] = grad[:, left]

    @pl.when(feat_ref[0] == 1)
    def _():
        out_ref[...] = value[:, right]
        grad_own[...] = grad[:, right]

    w_rows = w[pl.ds(lane, half), :]
    hid_ref[...] = lax.dot_general(
        grad, w_rows, (((1,), (1,)), ((), ())), preferred_element_type=F32
    ).astype(BF16)
    own = grad_own[...]
    gw_ref[0:256, :] = scale * lax.dot_general(
        agg[...], own, (((0,), (0,)), ((), ())), preferred_element_type=F32
    )
    eighths = jnp.sum(own.astype(F32).reshape(-1, 8, half), axis=0)
    gw_ref[256:264, :] = jnp.broadcast_to(
        scale * jnp.sum(eighths, axis=0, keepdims=True), (8, half)
    )


def middle(scale, feat, own, far, sides, far_sides, bias, far_bias):
    rows = own.shape[0]
    vmem = pl.BlockSpec(memory_space=pltpu.VMEM)
    return pl.pallas_call(
        functools.partial(middle_kernel, scale),
        out_shape=[
            jax.ShapeDtypeStruct((rows, EDGE), BF16),
            jax.ShapeDtypeStruct((rows, EDGE), BF16),
            jax.ShapeDtypeStruct((264, EDGE), F32),
        ],
        in_specs=[pl.BlockSpec(memory_space=pltpu.SMEM)] + [vmem] * 6,
        out_specs=[vmem] * 3,
        scratch_shapes=[
            pltpu.VMEM((rows, 256), BF16),
            pltpu.VMEM((256, 256), BF16),
            pltpu.VMEM((rows, 256), BF16),
            pltpu.VMEM((8, 256), F32),
            pltpu.VMEM((rows, EDGE), BF16),
        ],
        compiler_params=pltpu.CompilerParams(vmem_limit_bytes=VMEM_LIMIT),
        name="middle",
    )(feat, own, far, sides, far_sides, bias, far_bias)


def on_device(tile_vals, tile_rows, tile_cols, tile_count, features, weight, bias_term, cotangent):
    tiles = tile_vals[0, 0]
    rows = tile_rows[0, 0]
    cols = tile_cols[0, 0]
    local_rows = features.shape[0]
    my_zhi, my_x = lax.axis_index("zhi"), lax.axis_index("x")
    my_y, my_zlo = lax.axis_index("y"), lax.axis_index("zlo")
    feat = lax.axis_index("feat").reshape(1)
    node_total = local_rows * 128
    scale = 1.0 / math.sqrt(node_total)

    with jax.named_scope("gather_row"):
        z2, z1, z3 = [pull(features, "zhi", 4, k) for k in (2, 1, 3)]
    with jax.named_scope("sides"):
        sides = jnp.concatenate([cotangent, weight], axis=0)
        bias = jnp.broadcast_to(bias_term[None, :], (8, EDGE))
        far_sides = pull(sides, "feat", 2, 1)
        far_bias = pull(bias, "feat", 2, 1)
    z1, z2, z3, far_sides, far_bias = lax.optimization_barrier(
        (z1, z2, z3, far_sides, far_bias)
    )
    with jax.named_scope("gather_row"):
        near = jnp.concatenate([features, z1], axis=0)
        away = jnp.concatenate([z3, z2], axis=0)
        near_blocks = [near] + [pull(near, "x", 4, k) for k in (1, 2, 3)]
        away_blocks = [away] + [pull(away, "x", 4, k) for k in (1, 2, 3)]
    near_blocks[0], rows, cols = lax.optimization_barrier((near, rows, cols))

    per = local_rows // EDGE
    row_block, col_block = rows // per, cols // per
    rel_y, rel_zlo = (row_block // 2 - my_y) % 4, (row_block % 2 - my_zlo) % 2
    row_at = (rel_y * 2 + rel_zlo) * per + rows % per
    rel_zhi, rel_x = (col_block // 4 - my_zhi) % 4, (col_block % 4 - my_x) % 4
    second = rel_zhi >= 2
    inner = jnp.where(second, 3 - rel_zhi, rel_zhi)
    col_at = (rel_x * 2 + inner) * per + cols % per
    packed, totals = slot_lists(row_at, col_at, second, tile_count[0, 0])
    lists = [packed[0], packed[1]]
    counts = [totals[0:1], totals[1:2]]

    wide = [jax.ShapeDtypeStruct((HALF_TILES, EDGE, EDGE), F32)]
    block = [jax.ShapeDtypeStruct((local_rows, EDGE), BF16)] * 8
    pair = [jax.ShapeDtypeStruct((2 * local_rows, EDGE), BF16)] * 4
    (base,) = tile_pass(
        tiles, lists[0], counts[0], near_blocks, None, wide, False, "forward_near"
    )
    partial_sums = tile_pass(
        tiles, lists[1], counts[1], away_blocks, base, block, False, "forward_away"
    )

    with jax.named_scope("scatter_col"):
        mine = [partial_sums[0]]
        for k in range(1, 8):
            mine.append(push_col(partial_sums[k], k // 2, k % 2))
    own = sum_blocks(mine, BF16, "sum_col")
    far = pull(own, "feat", 2, 1)
    outputs, hidden, grads = middle(scale, feat, own, far, sides, far_sides, bias, far_bias)

    with jax.named_scope("gather_col"):
        beside = pull(hidden, "zlo", 2, 1)
        blocks = [hidden, beside]
        along = [pull(hidden, "y", 4, k) for k in (1, 2, 3)]
        others = [pull(beside, "y", 4, k) for k in (1, 2, 3)]
        for k in range(3):
            blocks += [along[k], others[k]]
    grads = pair_sum(grads, "zlo", 2, 1)
    blocks[1], grads = lax.optimization_barrier((blocks[1], grads))
    grads = pair_sum(grads, "x", 4, 1)
    grads = pair_sum(grads, "x", 4, 2)
    back_away = tile_pass(
        tiles, lists[1], counts[1], blocks, None, pair, True, "backward_away"
    )
    back_away, grads = lax.optimization_barrier((back_away, grads))
    with jax.named_scope("scatter_row_away"):
        got = [back_away[0]] + [push(back_away[k], "x", 4, k) for k in (1, 3, 2)]
    grads = pair_sum(grads, "zhi", 4, 1)
    near_count, got[1] = lax.optimization_barrier((counts[0], got[1]))
    back_near = tile_pass(tiles, lists[0], near_count, blocks, None, pair, True, "backward_near")
    *got, back_near, grads = lax.optimization_barrier((*got, back_near, grads))
    grads = pair_sum(grads, "zhi", 4, 2)
    z3, z2 = sum_pair(got, (BF16, BF16), "sum_away")
    z2, z3, back_near = lax.optimization_barrier((z2, z3, back_near))
    with jax.named_scope("scatter_row_near"):
        near_got = [back_near[0]] + [push(back_near[k], "x", 4, k) for k in (1, 3, 2)]
    with jax.named_scope("scatter_row_away"):
        z2, z3 = push(z2, "zhi", 4, 2), push(z3, "zhi", 4, 3)
    near_got[1], grads = lax.optimization_barrier((near_got[1], grads))
    grads = pair_sum(grads, "y", 4, 1)
    *near_got, z2, z3 = lax.optimization_barrier((*near_got, z2, z3))
    z0, z1 = sum_pair(near_got, (F32, BF16), "sum_near")
    with jax.named_scope("scatter_row_near"):
        z1 = push(z1, "zhi", 4, 1)
    grads = pair_sum(grads, "y", 4, 2)

    grad_feat = sum_blocks([z0, z1, z2, z3], BF16, "sum_z")
    return outputs, grad_feat, grads[:256], grads[256]


def solution(mesh):
    fine = Mesh(mesh.devices.reshape(4, 4, 4, 2, 2), ("zhi", "x", "y", "zlo", "feat"))
    row, col = ("zhi", "x"), ("y", "zlo")
    nodes = P(row + col, "feat")
    return jax.shard_map(
        on_device,
        mesh=fine,
        in_specs=(
            P(row, col, None, None, None),
            P(row, col, None),
            P(row, col, None),
            P(row, col),
            nodes,
            P(None, "feat"),
            P("feat"),
            nodes,
        ),
        out_specs=(nodes, nodes, P(None, "feat"), P("feat")),
        check_vma=False,
    )
```

```python
import functools
import math

import jax
import jax.numpy as jnp
from jax import lax
from jax.experimental import pallas as pl
from jax.experimental.pallas import tpu as pltpu
from jax.sharding import Mesh
from jax.sharding import PartitionSpec as P

BF16 = jnp.bfloat16
F32 = jnp.float32
EDGE = 128
CHUNK = 32
DEPTH = 3
HALF_TILES = 32
VMEM_LIMIT = 40 * 2**20


def pull(value, axis, size, step):
    return lax.ppermute(value, axis, [((i + step) % size, i) for i in range(size)])


def push(value, axis, size, step):
    return lax.ppermute(value, axis, [(i, (i + step) % size) for i in range(size)])


def push_col(value, step_y, step_z):
    pairs = []
    for y in range(4):
        for z in range(2):
            pairs.append((y * 2 + z, ((y + step_y) % 4) * 2 + (z + step_z) % 2))
    return lax.ppermute(value, ("y", "zlo"), pairs)


def group_sum(value, axis, size):
    with jax.named_scope("weight_grads"):
        parts = [pull(value, axis, size, k) for k in (1, 2, 3)]
        return (value + parts[1]) + (parts[0] + parts[2])


def pair_sum(value, axis, size, flip):
    with jax.named_scope("weight_grads"):
        return value + lax.ppermute(value, axis, [(i, i ^ flip) for i in range(size)])


def slot_lists(rows, cols, second, live):
    slots = rows.shape[0]
    index = jnp.arange(slots, dtype=jnp.int32)
    code = index * 4096 + rows * 64 + cols
    kind = jnp.stack([jnp.logical_not(second), second]) & (index < live)[None]
    before = index[None, :] < index[:, None]
    rank = jnp.sum((kind[:, None, :] & before[None]).astype(jnp.int32), axis=2)
    hit = kind[:, None, :] & (rank[:, None, :] == index[None, :, None])
    packed = jnp.sum(jnp.where(hit, code[None, None, :], 0), axis=2)
    totals = jnp.sum(kind.astype(jnp.int32), axis=1)
    packed = jnp.where(index[None] < totals[:, None], packed, 32 * 64 + 32)
    return packed, totals


def tile_kernel(transpose, n_src, n_out, has_base, total_ref, list_ref, tiles_hbm, *refs):
    src_refs = refs[:n_src]
    base = refs[n_src] if has_base else None
    n_in = n_src + has_base
    out_refs = refs[n_in : n_in + n_out]
    buf, sem, source, acc = refs[n_in + n_out :]
    chunks = (total_ref[0] + CHUNK - 1) // CHUNK

    def fetch(index):
        slot = lax.rem(index, DEPTH)
        for k in range(CHUNK):
            code = list_ref[index * CHUNK + k]
            pltpu.make_async_copy(
                tiles_hbm.at[lax.shift_right_logical(code, 12)], buf.at[slot, k], sem.at[slot]
            ).start()

    for k in range(DEPTH - 1):

        @pl.when(k < chunks)
        def _():
            fetch(jnp.int32(k))

    per = src_refs[0].shape[0] // EDGE
    for k in range(n_src):
        source[k * per : (k + 1) * per] = src_refs[k][...].reshape(per, EDGE, EDGE)
    source[n_src * per] = jnp.zeros((EDGE, EDGE), BF16)
    acc[...] = jnp.zeros_like(acc)

    def one_chunk(index, carry):
        slot = lax.rem(index, DEPTH)

        @pl.when(index + DEPTH - 1 < chunks)
        def _():
            fetch(index + DEPTH - 1)

        pltpu.make_async_copy(tiles_hbm.at[pl.ds(0, CHUNK)], buf.at[slot], sem.at[slot]).wait()
        for k in range(CHUNK):
            code = list_ref[index * CHUNK + k]
            row_at = lax.shift_right_logical(code, 6) & 63
            col_at = code & 63
            out_at, src_at = (col_at, row_at) if transpose else (row_at, col_at)
            dims = (((0,), (0,)), ((), ())) if transpose else (((1,), (0,)), ((), ()))
            acc[out_at] += lax.dot_general(
                buf[slot, k], source[src_at], dims, preferred_element_type=F32
            )
        return carry

    lax.fori_loop(0, chunks, one_chunk, 0)
    if out_refs[0].dtype == F32:
        out_refs[0][...] = acc[0:HALF_TILES]
        return
    per = out_refs[0].shape[0] // EDGE
    for k in range(n_out):
        total = acc[k * per : (k + 1) * per]
        if has_base:
            total = total + base[k * per : (k + 1) * per]
        out_refs[k][...] = total.reshape(per * EDGE, EDGE).astype(BF16)


def tile_pass(tiles, packed, total, sources, base, out_shape, transpose, name):
    smem = pl.BlockSpec(memory_space=pltpu.SMEM)
    vmem = pl.BlockSpec(memory_space=pltpu.VMEM)
    inputs = list(sources) + ([] if base is None else [base])
    return pl.pallas_call(
        functools.partial(
            tile_kernel, transpose, len(sources), len(out_shape), int(base is not None)
        ),
        out_shape=out_shape,
        in_specs=[smem, smem, pl.BlockSpec(memory_space=pl.ANY)] + [vmem] * len(inputs),
        out_specs=[vmem] * len(out_shape),
        scratch_shapes=[
            pltpu.VMEM((DEPTH, CHUNK, EDGE, EDGE), BF16),
            pltpu.SemaphoreType.DMA((DEPTH,)),
            pltpu.VMEM((HALF_TILES + 1, EDGE, EDGE), BF16),
            pltpu.VMEM((HALF_TILES + 1, EDGE, EDGE), F32),
        ],
        compiler_params=pltpu.CompilerParams(vmem_limit_bytes=VMEM_LIMIT),
        cost_estimate=pl.CostEstimate(
            flops=2 * tiles.size * EDGE, bytes_accessed=2 * tiles.size, transcendentals=0
        ),
        name=name,
    )(total, packed, tiles, *inputs)


def sum_kernel(*refs):
    total = refs[0][...].astype(F32)
    for ref in refs[1:-1]:
        total = total + ref[...].astype(F32)
    refs[-1][...] = total.astype(refs[-1].dtype)


def sum_blocks(blocks, dtype, name):
    vmem = pl.BlockSpec(memory_space=pltpu.VMEM)
    return pl.pallas_call(
        sum_kernel,
        out_shape=jax.ShapeDtypeStruct(blocks[0].shape, dtype),
        in_specs=[vmem] * len(blocks),
        out_specs=vmem,
        compiler_params=pltpu.CompilerParams(vmem_limit_bytes=VMEM_LIMIT),
        name=name,
    )(*blocks)


def sum_pair_kernel(*refs):
    total = refs[0][...].astype(F32)
    for ref in refs[1:-2]:
        total = total + ref[...].astype(F32)
    rows = refs[-1].shape[0]
    refs[-2][...] = total[:rows].astype(refs[-2].dtype)
    refs[-1][...] = total[rows:].astype(refs[-1].dtype)


def sum_pair(blocks, dtypes, name):
    vmem = pl.BlockSpec(memory_space=pltpu.VMEM)
    rows, width = blocks[0].shape
    return pl.pallas_call(
        sum_pair_kernel,
        out_shape=[jax.ShapeDtypeStruct((rows // 2, width), d) for d in dtypes],
        in_specs=[vmem] * len(blocks),
        out_specs=[vmem] * 2,
        compiler_params=pltpu.CompilerParams(vmem_limit_bytes=VMEM_LIMIT),
        name=name,
    )(*blocks)


def middle_kernel(
    scale, feat_ref, own_ref, far_ref, sides_ref, far_sides_ref, bias_ref, far_bias_ref,
    out_ref, hid_ref, gw_ref, agg, w, cot, bias, grad_own,
):
    half = EDGE
    rows = own_ref.shape[0]

    def place(here, there):
        agg[:, here] = own_ref[...]
        agg[:, there] = far_ref[...]
        cot[:, here] = sides_ref[0:rows, :]
        cot[:, there] = far_sides_ref[0:rows, :]
        w[:, here] = sides_ref[rows:, :]
        w[:, there] = far_sides_ref[rows:, :]
        bias[:, here] = bias_ref[...]
        bias[:, there] = far_bias_ref[...]

    left, right = slice(0, half), slice(half, 2 * half)

    @pl.when(feat_ref[0] == 0)
    def _():
        place(left, right)

    @pl.when(feat_ref[0] == 1)
    def _():
        place(right, left)

    lane = pl.multiple_of(feat_ref[0] * half, half)
    pre = jnp.dot(agg[...], w[...], preferred_element_type=F32) + bias[0:1, :]
    sig = jax.nn.sigmoid(pre)
    value = (pre * sig).astype(BF16)
    slope = sig * (1.0 + pre * (1.0 - sig))
    grad = (cot[...].astype(F32) * slope).astype(BF16)

    @pl.when(feat_ref[0] == 0)
    def _():
        out_ref[...] = value[:, left]
        grad_own[...] = grad[:, left]

    @pl.when(feat_ref[0] == 1)
    def _():
        out_ref[...] = value[:, right]
        grad_own[...] = grad[:, right]

    w_rows = w[pl.ds(lane, half), :]
    hid_ref[...] = lax.dot_general(
        grad, w_rows, (((1,), (1,)), ((), ())), preferred_element_type=F32
    ).astype(BF16)
    own = grad_own[...]
    gw_ref[0:256, :] = scale * lax.dot_general(
        agg[...], own, (((0,), (0,)), ((), ())), preferred_element_type=F32
    )
    eighths = jnp.sum(own.astype(F32).reshape(-1, 8, half), axis=0)
    gw_ref[256:264, :] = jnp.broadcast_to(
        scale * jnp.sum(eighths, axis=0, keepdims=True), (8, half)
    )


def middle(scale, feat, own, far, sides, far_sides, bias, far_bias):
    rows = own.shape[0]
    vmem = pl.BlockSpec(memory_space=pltpu.VMEM)
    return pl.pallas_call(
        functools.partial(middle_kernel, scale),
        out_shape=[
            jax.ShapeDtypeStruct((rows, EDGE), BF16),
            jax.ShapeDtypeStruct((rows, EDGE), BF16),
            jax.ShapeDtypeStruct((264, EDGE), F32),
        ],
        in_specs=[pl.BlockSpec(memory_space=pltpu.SMEM)] + [vmem] * 6,
        out_specs=[vmem] * 3,
        scratch_shapes=[
            pltpu.VMEM((rows, 256), BF16),
            pltpu.VMEM((256, 256), BF16),
            pltpu.VMEM((rows, 256), BF16),
            pltpu.VMEM((8, 256), F32),
            pltpu.VMEM((rows, EDGE), BF16),
        ],
        compiler_params=pltpu.CompilerParams(vmem_limit_bytes=VMEM_LIMIT),
        name="middle",
    )(feat, own, far, sides, far_sides, bias, far_bias)


def on_device(tile_vals, tile_rows, tile_cols, tile_count, features, weight, bias_term, cotangent):
    tiles = tile_vals[0, 0]
    rows = tile_rows[0, 0]
    cols = tile_cols[0, 0]
    local_rows = features.shape[0]
    my_zhi, my_x = lax.axis_index("zhi"), lax.axis_index("x")
    my_y, my_zlo = lax.axis_index("y"), lax.axis_index("zlo")
    feat = lax.axis_index("feat").reshape(1)
    node_total = local_rows * 128
    scale = 1.0 / math.sqrt(node_total)

    with jax.named_scope("gather_row"):
        z2, z1, z3 = [pull(features, "zhi", 4, k) for k in (2, 1, 3)]
    with jax.named_scope("sides"):
        sides = jnp.concatenate([cotangent, weight], axis=0)
        bias = jnp.broadcast_to(bias_term[None, :], (8, EDGE))
        far_sides = pull(sides, "feat", 2, 1)
        far_bias = pull(bias, "feat", 2, 1)
    z1, z2, z3, far_sides, far_bias = lax.optimization_barrier(
        (z1, z2, z3, far_sides, far_bias)
    )
    with jax.named_scope("gather_row"):
        near = jnp.concatenate([features, z1], axis=0)
        away = jnp.concatenate([z3, z2], axis=0)
        near_blocks = [near] + [pull(near, "x", 4, k) for k in (1, 2, 3)]
        away_blocks = [away] + [pull(away, "x", 4, k) for k in (1, 2, 3)]
    near_blocks[0], rows, cols = lax.optimization_barrier((near, rows, cols))

    per = local_rows // EDGE
    row_block, col_block = rows // per, cols // per
    rel_y, rel_zlo = (row_block // 2 - my_y) % 4, (row_block % 2 - my_zlo) % 2
    row_at = (rel_y * 2 + rel_zlo) * per + rows % per
    rel_zhi, rel_x = (col_block // 4 - my_zhi) % 4, (col_block % 4 - my_x) % 4
    second = rel_zhi >= 2
    inner = jnp.where(second, 3 - rel_zhi, rel_zhi)
    col_at = (rel_x * 2 + inner) * per + cols % per
    packed, totals = slot_lists(row_at, col_at, second, tile_count[0, 0])
    lists = [packed[0], packed[1]]
    counts = [totals[0:1], totals[1:2]]

    wide = [jax.ShapeDtypeStruct((HALF_TILES, EDGE, EDGE), F32)]
    block = [jax.ShapeDtypeStruct((local_rows, EDGE), BF16)] * 8
    pair = [jax.ShapeDtypeStruct((2 * local_rows, EDGE), BF16)] * 4
    (base,) = tile_pass(
        tiles, lists[0], counts[0], near_blocks, None, wide, False, "forward_near"
    )
    partial_sums = tile_pass(
        tiles, lists[1], counts[1], away_blocks, base, block, False, "forward_away"
    )

    with jax.named_scope("scatter_col"):
        mine = [partial_sums[0]]
        for k in range(1, 8):
            mine.append(push_col(partial_sums[k], k // 2, k % 2))
    own = sum_blocks(mine, BF16, "sum_col")
    far = pull(own, "feat", 2, 1)
    outputs, hidden, grads = middle(scale, feat, own, far, sides, far_sides, bias, far_bias)

    with jax.named_scope("gather_col"):
        beside = pull(hidden, "zlo", 2, 1)
        blocks = [hidden, beside]
        along = [pull(hidden, "y", 4, k) for k in (1, 2, 3)]
        others = [pull(beside, "y", 4, k) for k in (1, 2, 3)]
        for k in range(3):
            blocks += [along[k], others[k]]
    grads = pair_sum(grads, "zlo", 2, 1)
    grads = group_sum(grads, "x", 4)
    back_away = tile_pass(
        tiles, lists[1], counts[1], blocks, None, pair, True, "backward_away"
    )
    back_away, grads = lax.optimization_barrier((back_away, grads))
    with jax.named_scope("scatter_row_away"):
        got = [back_away[0]] + [push(back_away[k], "x", 4, k) for k in (1, 3, 2)]
    grads = pair_sum(grads, "zhi", 4, 1)
    near_count, got[1] = lax.optimization_barrier((counts[0], got[1]))
    back_near = tile_pass(tiles, lists[0], near_count, blocks, None, pair, True, "backward_near")
    *got, back_near, grads = lax.optimization_barrier((*got, back_near, grads))
    grads = pair_sum(grads, "zhi", 4, 2)
    z3, z2 = sum_pair(got, (BF16, BF16), "sum_away")
    z2, z3, back_near = lax.optimization_barrier((z2, z3, back_near))
    with jax.named_scope("scatter_row_near"):
        near_got = [back_near[0]] + [push(back_near[k], "x", 4, k) for k in (1, 3, 2)]
    with jax.named_scope("scatter_row_away"):
        z2, z3 = push(z2, "zhi", 4, 2), push(z3, "zhi", 4, 3)
    near_got[1], grads = lax.optimization_barrier((near_got[1], grads))
    grads = group_sum(grads, "y", 4)
    z0, z1 = sum_pair(near_got, (F32, BF16), "sum_near")
    with jax.named_scope("scatter_row_near"):
        z1 = push(z1, "zhi", 4, 1)

    grad_feat = sum_blocks([z0, z1, z2, z3], BF16, "sum_z")
    return outputs, grad_feat, grads[:256], grads[256]


def solution(mesh):
    fine = Mesh(mesh.devices.reshape(4, 4, 4, 2, 2), ("zhi", "x", "y", "zlo", "feat"))
    row, col = ("zhi", "x"), ("y", "zlo")
    nodes = P(row + col, "feat")
    return jax.shard_map(
        on_device,
        mesh=fine,
        in_specs=(
            P(row, col, None, None, None),
            P(row, col, None),
            P(row, col, None),
            P(row, col),
            nodes,
            P(None, "feat"),
            P("feat"),
            nodes,
        ),
        out_specs=(nodes, nodes, P(None, "feat"), P("feat")),
        check_vma=False,
    )
```

```python
import functools
import math

import jax
import jax.numpy as jnp
from jax import lax
from jax.experimental import pallas as pl
from jax.experimental.pallas import tpu as pltpu
from jax.sharding import Mesh
from jax.sharding import PartitionSpec as P

BF16 = jnp.bfloat16
F32 = jnp.float32
EDGE = 128
CHUNK = 32
DEPTH = 3
HALF_TILES = 32
VMEM_LIMIT = 40 * 2**20


def pull(value, axis, size, step):
    return lax.ppermute(value, axis, [((i + step) % size, i) for i in range(size)])


def push(value, axis, size, step):
    return lax.ppermute(value, axis, [(i, (i + step) % size) for i in range(size)])


def push_col(value, step_y, step_z):
    pairs = []
    for y in range(4):
        for z in range(2):
            pairs.append((y * 2 + z, ((y + step_y) % 4) * 2 + (z + step_z) % 2))
    return lax.ppermute(value, ("y", "zlo"), pairs)


def group_sum(value, axis, size):
    with jax.named_scope("weight_grads"):
        parts = [pull(value, axis, size, k) for k in (1, 2, 3)]
        return (value + parts[1]) + (parts[0] + parts[2])


def pair_sum(value, axis, size, flip):
    with jax.named_scope("weight_grads"):
        return value + lax.ppermute(value, axis, [(i, i ^ flip) for i in range(size)])


def slot_lists(rows, cols, second, live):
    slots = rows.shape[0]
    index = jnp.arange(slots, dtype=jnp.int32)
    code = index * 4096 + rows * 64 + cols
    kind = jnp.stack([jnp.logical_not(second), second]) & (index < live)[None]
    before = index[None, :] < index[:, None]
    rank = jnp.sum((kind[:, None, :] & before[None]).astype(jnp.int32), axis=2)
    hit = kind[:, None, :] & (rank[:, None, :] == index[None, :, None])
    packed = jnp.sum(jnp.where(hit, code[None, None, :], 0), axis=2)
    totals = jnp.sum(kind.astype(jnp.int32), axis=1)
    packed = jnp.where(index[None] < totals[:, None], packed, 32 * 64 + 32)
    return packed, totals


def tile_kernel(transpose, n_src, n_out, has_base, total_ref, list_ref, tiles_hbm, *refs):
    src_refs = refs[:n_src]
    base = refs[n_src] if has_base else None
    n_in = n_src + has_base
    out_refs = refs[n_in : n_in + n_out]
    buf, sem, source, acc = refs[n_in + n_out :]
    chunks = (total_ref[0] + CHUNK - 1) // CHUNK

    def fetch(index):
        slot = lax.rem(index, DEPTH)
        for k in range(CHUNK):
            code = list_ref[index * CHUNK + k]
            pltpu.make_async_copy(
                tiles_hbm.at[lax.shift_right_logical(code, 12)], buf.at[slot, k], sem.at[slot]
            ).start()

    for k in range(DEPTH - 1):

        @pl.when(k < chunks)
        def _():
            fetch(jnp.int32(k))

    per = src_refs[0].shape[0] // EDGE
    for k in range(n_src):
        source[k * per : (k + 1) * per] = src_refs[k][...].reshape(per, EDGE, EDGE)
    source[n_src * per] = jnp.zeros((EDGE, EDGE), BF16)
    acc[...] = jnp.zeros_like(acc)

    def one_chunk(index, carry):
        slot = lax.rem(index, DEPTH)

        @pl.when(index + DEPTH - 1 < chunks)
        def _():
            fetch(index + DEPTH - 1)

        pltpu.make_async_copy(tiles_hbm.at[pl.ds(0, CHUNK)], buf.at[slot], sem.at[slot]).wait()
        for k in range(CHUNK):
            code = list_ref[index * CHUNK + k]
            row_at = lax.shift_right_logical(code, 6) & 63
            col_at = code & 63
            out_at, src_at = (col_at, row_at) if transpose else (row_at, col_at)
            dims = (((0,), (0,)), ((), ())) if transpose else (((1,), (0,)), ((), ()))
            acc[out_at] += lax.dot_general(
                buf[slot, k], source[src_at], dims, preferred_element_type=F32
            )
        return carry

    lax.fori_loop(0, chunks, one_chunk, 0)
    if out_refs[0].dtype == F32:
        out_refs[0][...] = acc[0:HALF_TILES]
        return
    per = out_refs[0].shape[0] // EDGE
    for k in range(n_out):
        total = acc[k * per : (k + 1) * per]
        if has_base:
            total = total + base[k * per : (k + 1) * per]
        out_refs[k][...] = total.reshape(per * EDGE, EDGE).astype(BF16)


def tile_pass(tiles, packed, total, sources, base, out_shape, transpose, name):
    smem = pl.BlockSpec(memory_space=pltpu.SMEM)
    vmem = pl.BlockSpec(memory_space=pltpu.VMEM)
    inputs = list(sources) + ([] if base is None else [base])
    return pl.pallas_call(
        functools.partial(
            tile_kernel, transpose, len(sources), len(out_shape), int(base is not None)
        ),
        out_shape=out_shape,
        in_specs=[smem, smem, pl.BlockSpec(memory_space=pl.ANY)] + [vmem] * len(inputs),
        out_specs=[vmem] * len(out_shape),
        scratch_shapes=[
            pltpu.VMEM((DEPTH, CHUNK, EDGE, EDGE), BF16),
            pltpu.SemaphoreType.DMA((DEPTH,)),
            pltpu.VMEM((HALF_TILES + 1, EDGE, EDGE), BF16),
            pltpu.VMEM((HALF_TILES + 1, EDGE, EDGE), F32),
        ],
        compiler_params=pltpu.CompilerParams(vmem_limit_bytes=VMEM_LIMIT),
        cost_estimate=pl.CostEstimate(
            flops=2 * tiles.size * EDGE, bytes_accessed=2 * tiles.size, transcendentals=0
        ),
        name=name,
    )(total, packed, tiles, *inputs)


def sum_kernel(*refs):
    total = refs[0][...].astype(F32)
    for ref in refs[1:-1]:
        total = total + ref[...].astype(F32)
    refs[-1][...] = total.astype(refs[-1].dtype)


def sum_blocks(blocks, dtype, name):
    vmem = pl.BlockSpec(memory_space=pltpu.VMEM)
    return pl.pallas_call(
        sum_kernel,
        out_shape=jax.ShapeDtypeStruct(blocks[0].shape, dtype),
        in_specs=[vmem] * len(blocks),
        out_specs=vmem,
        compiler_params=pltpu.CompilerParams(vmem_limit_bytes=VMEM_LIMIT),
        name=name,
    )(*blocks)


def sum_pair_kernel(*refs):
    total = refs[0][...].astype(F32)
    for ref in refs[1:-2]:
        total = total + ref[...].astype(F32)
    rows = refs[-1].shape[0]
    refs[-2][...] = total[:rows].astype(refs[-2].dtype)
    refs[-1][...] = total[rows:].astype(refs[-1].dtype)


def sum_pair(blocks, dtypes, name):
    vmem = pl.BlockSpec(memory_space=pltpu.VMEM)
    rows, width = blocks[0].shape
    return pl.pallas_call(
        sum_pair_kernel,
        out_shape=[jax.ShapeDtypeStruct((rows // 2, width), d) for d in dtypes],
        in_specs=[vmem] * len(blocks),
        out_specs=[vmem] * 2,
        compiler_params=pltpu.CompilerParams(vmem_limit_bytes=VMEM_LIMIT),
        name=name,
    )(*blocks)


def middle_kernel(
    scale, feat_ref, own_ref, far_ref, sides_ref, far_sides_ref, bias_ref, far_bias_ref,
    out_ref, hid_ref, gw_ref, agg, w, cot, bias, grad_own,
):
    half = EDGE
    rows = own_ref.shape[0]

    def place(here, there):
        agg[:, here] = own_ref[...]
        agg[:, there] = far_ref[...]
        cot[:, here] = sides_ref[0:rows, :]
        cot[:, there] = far_sides_ref[0:rows, :]
        w[:, here] = sides_ref[rows:, :]
        w[:, there] = far_sides_ref[rows:, :]
        bias[:, here] = bias_ref[...]
        bias[:, there] = far_bias_ref[...]

    left, right = slice(0, half), slice(half, 2 * half)

    @pl.when(feat_ref[0] == 0)
    def _():
        place(left, right)

    @pl.when(feat_ref[0] == 1)
    def _():
        place(right, left)

    lane = pl.multiple_of(feat_ref[0] * half, half)
    pre = jnp.dot(agg[...], w[...], preferred_element_type=F32) + bias[0:1, :]
    sig = jax.nn.sigmoid(pre)
    value = (pre * sig).astype(BF16)
    slope = sig * (1.0 + pre * (1.0 - sig))
    grad = (cot[...].astype(F32) * slope).astype(BF16)

    @pl.when(feat_ref[0] == 0)
    def _():
        out_ref[...] = value[:, left]
        grad_own[...] = grad[:, left]

    @pl.when(feat_ref[0] == 1)
    def _():
        out_ref[...] = value[:, right]
        grad_own[...] = grad[:, right]

    w_rows = w[pl.ds(lane, half), :]
    hid_ref[...] = lax.dot_general(
        grad, w_rows, (((1,), (1,)), ((), ())), preferred_element_type=F32
    ).astype(BF16)
    own = grad_own[...]
    gw_ref[0:256, :] = scale * lax.dot_general(
        agg[...], own, (((0,), (0,)), ((), ())), preferred_element_type=F32
    )
    eighths = jnp.sum(own.astype(F32).reshape(-1, 8, half), axis=0)
    gw_ref[256:264, :] = jnp.broadcast_to(
        scale * jnp.sum(eighths, axis=0, keepdims=True), (8, half)
    )


def middle(scale, feat, own, far, sides, far_sides, bias, far_bias):
    rows = own.shape[0]
    vmem = pl.BlockSpec(memory_space=pltpu.VMEM)
    return pl.pallas_call(
        functools.partial(middle_kernel, scale),
        out_shape=[
            jax.ShapeDtypeStruct((rows, EDGE), BF16),
            jax.ShapeDtypeStruct((rows, EDGE), BF16),
            jax.ShapeDtypeStruct((264, EDGE), F32),
        ],
        in_specs=[pl.BlockSpec(memory_space=pltpu.SMEM)] + [vmem] * 6,
        out_specs=[vmem] * 3,
        scratch_shapes=[
            pltpu.VMEM((rows, 256), BF16),
            pltpu.VMEM((256, 256), BF16),
            pltpu.VMEM((rows, 256), BF16),
            pltpu.VMEM((8, 256), F32),
            pltpu.VMEM((rows, EDGE), BF16),
        ],
        compiler_params=pltpu.CompilerParams(vmem_limit_bytes=VMEM_LIMIT),
        name="middle",
    )(feat, own, far, sides, far_sides, bias, far_bias)


def on_device(tile_vals, tile_rows, tile_cols, tile_count, features, weight, bias_term, cotangent):
    tiles = tile_vals[0, 0]
    rows = tile_rows[0, 0]
    cols = tile_cols[0, 0]
    local_rows = features.shape[0]
    my_zhi, my_x = lax.axis_index("zhi"), lax.axis_index("x")
    my_y, my_zlo = lax.axis_index("y"), lax.axis_index("zlo")
    feat = lax.axis_index("feat").reshape(1)
    node_total = local_rows * 128
    scale = 1.0 / math.sqrt(node_total)

    with jax.named_scope("gather_row"):
        z2, z1, z3 = [pull(features, "zhi", 4, k) for k in (2, 1, 3)]
    with jax.named_scope("sides"):
        sides = jnp.concatenate([cotangent, weight], axis=0)
        bias = jnp.broadcast_to(bias_term[None, :], (8, EDGE))
        far_sides = pull(sides, "feat", 2, 1)
        far_bias = pull(bias, "feat", 2, 1)
    z1, z2, z3, far_sides, far_bias = lax.optimization_barrier(
        (z1, z2, z3, far_sides, far_bias)
    )
    with jax.named_scope("gather_row"):
        near = jnp.concatenate([features, z1], axis=0)
        away = jnp.concatenate([z3, z2], axis=0)
        near_blocks = [near] + [pull(near, "x", 4, k) for k in (1, 2, 3)]
        away_blocks = [away] + [pull(away, "x", 4, k) for k in (1, 2, 3)]
    near_blocks[0], rows, cols = lax.optimization_barrier((near, rows, cols))

    per = local_rows // EDGE
    row_block, col_block = rows // per, cols // per
    rel_y, rel_zlo = (row_block // 2 - my_y) % 4, (row_block % 2 - my_zlo) % 2
    row_at = (rel_y * 2 + rel_zlo) * per + rows % per
    rel_zhi, rel_x = (col_block // 4 - my_zhi) % 4, (col_block % 4 - my_x) % 4
    second = rel_zhi >= 2
    inner = jnp.where(second, 3 - rel_zhi, rel_zhi)
    col_at = (rel_x * 2 + inner) * per + cols % per
    packed, totals = slot_lists(row_at, col_at, second, tile_count[0, 0])
    lists = [packed[0], packed[1]]
    counts = [totals[0:1], totals[1:2]]

    wide = [jax.ShapeDtypeStruct((HALF_TILES, EDGE, EDGE), F32)]
    block = [jax.ShapeDtypeStruct((local_rows, EDGE), BF16)] * 8
    pair = [jax.ShapeDtypeStruct((2 * local_rows, EDGE), BF16)] * 4
    (base,) = tile_pass(
        tiles, lists[0], counts[0], near_blocks, None, wide, False, "forward_near"
    )
    partial_sums = tile_pass(
        tiles, lists[1], counts[1], away_blocks, base, block, False, "forward_away"
    )

    with jax.named_scope("scatter_col"):
        mine = [partial_sums[0]]
        for k in range(1, 8):
            mine.append(push_col(partial_sums[k], k // 2, k % 2))
    own = sum_blocks(mine, BF16, "sum_col")
    far = pull(own, "feat", 2, 1)
    outputs, hidden, grads = middle(scale, feat, own, far, sides, far_sides, bias, far_bias)

    with jax.named_scope("gather_col"):
        beside = pull(hidden, "zlo", 2, 1)
        blocks = [hidden, beside]
        along = [pull(hidden, "y", 4, k) for k in (1, 2, 3)]
        others = [pull(beside, "y", 4, k) for k in (1, 2, 3)]
        for k in range(3):
            blocks += [along[k], others[k]]
    grads = pair_sum(grads, "zlo", 2, 1)
    grads = group_sum(grads, "x", 4)
    back_away = tile_pass(
        tiles, lists[1], counts[1], blocks, None, pair, True, "backward_away"
    )
    back_away, grads = lax.optimization_barrier((back_away, grads))
    with jax.named_scope("scatter_row_away"):
        got = [back_away[0]] + [push(back_away[k], "x", 4, k) for k in (1, 3, 2)]
    grads = pair_sum(grads, "zhi", 4, 1)
    near_count, got[1], grads = lax.optimization_barrier((counts[0], got[1], grads))
    grads = pair_sum(grads, "zhi", 4, 2)
    back_near = tile_pass(tiles, lists[0], near_count, blocks, None, pair, True, "backward_near")
    *got, back_near, grads = lax.optimization_barrier((*got, back_near, grads))
    z3, z2 = sum_pair(got, (BF16, BF16), "sum_away")
    z2, z3, back_near = lax.optimization_barrier((z2, z3, back_near))
    with jax.named_scope("scatter_row_near"):
        near_got = [back_near[0]] + [push(back_near[k], "x", 4, k) for k in (1, 3, 2)]
    with jax.named_scope("scatter_row_away"):
        z2, z3 = push(z2, "zhi", 4, 2), push(z3, "zhi", 4, 3)
    near_got[1], grads = lax.optimization_barrier((near_got[1], grads))
    grads = group_sum(grads, "y", 4)
    z0, z1 = sum_pair(near_got, (F32, BF16), "sum_near")
    with jax.named_scope("scatter_row_near"):
        z1 = push(z1, "zhi", 4, 1)

    grad_feat = sum_blocks([z0, z1, z2, z3], BF16, "sum_z")
    return outputs, grad_feat, grads[:256], grads[256]


def solution(mesh):
    fine = Mesh(mesh.devices.reshape(4, 4, 4, 2, 2), ("zhi", "x", "y", "zlo", "feat"))
    row, col = ("zhi", "x"), ("y", "zlo")
    nodes = P(row + col, "feat")
    return jax.shard_map(
        on_device,
        mesh=fine,
        in_specs=(
            P(row, col, None, None, None),
            P(row, col, None),
            P(row, col, None),
            P(row, col),
            nodes,
            P(None, "feat"),
            P("feat"),
            nodes,
        ),
        out_specs=(nodes, nodes, P(None, "feat"), P("feat")),
        check_vma=False,
    )
```
